256 devices in a mesh: lat: 8 (over y, core), lon: 32 (over x, z).
Axes of the slice: x: 4, y: 4, z: 8, core: 2. Of those that a mesh axis runs over, the one named last changes fastest.
Arguments:
- x_field: float32 [8, 32, 128, 512], P('lat', 'lon'), may hold values from -6 to 6
- residual: float32 [8, 32, 128, 512], P('lat', 'lon'), may hold values from -120 to 120
- direction: float32 [8, 32, 128, 512], P('lat', 'lon'), may hold values from -120 to 120
- a_node: bfloat16 [8, 32, 128, 512], P('lat', 'lon'), may hold values from -6 to 6
- a_edge: bfloat16 [8, 32, 1024, 512], P('lat', 'lon'), may hold values from -6 to 6
- senders: int32 [8, 32, 1024], P('lat', 'lon'), may hold values from -1 to 1151, as said below
- receivers: int32 [8, 32, 1024], P('lat', 'lon'), may hold values from -1 to 127, as said below
- obs_weight: float32 [8, 32, 128], P('lat', 'lon'), may hold values from 0.5 to 4
- w_send: bfloat16 [512, 512], replicated, may hold values from -0.25 to 0.25
- w_recv: bfloat16 [512, 512], replicated, may hold values from -0.25 to 0.25
- w_edge_out: bfloat16 [512, 512], replicated, may hold values from -0.25 to 0.25
- w_node_self: bfloat16 [512, 512], replicated, may hold values from -0.25 to 0.25
- w_node_msg: bfloat16 [512, 512], replicated, may hold values from -0.25 to 0.25
- w_node_out: bfloat16 [512, 512], replicated, may hold values from -0.25 to 0.25
Outputs:
- new_field: float32 [8, 32, 128, 512], P('lat', 'lon')
- new_residual: float32 [8, 32, 128, 512], P('lat', 'lon')
- new_direction: float32 [8, 32, 128, 512], P('lat', 'lon')
The draws below stay inside these ranges and needn't reach their ends.
Inputs may be any that keep to these rules, and one draw needn't show every extreme that they name: `senders`: -1 marks a padded slot, exactly where receivers is -1; in each region the live slots come first; otherwise s // 128 is a block of the 3 x 3 neighbourhood whose latitude offset stays inside the mesh, and some region has no padded slot. `receivers`: -1 exactly at padded slots.
All inputs are finite; a program needn't handle non-finite values.
Results may differ from the reference program's by a relative error of at most 0.008.
Values may be sent and summed in bfloat16 or wider, within the bound.
No kernel may reach another device: no remote copies, remote signals or barrier semaphores. Data moves between devices by JAX's collectives and lax.ppermute only.
A program may use at most 64 MiB of HBM per device.

```python
import math
import jax
import jax.numpy as jnp
from jax import lax

LATENT = 512
NODE_DEV = 128
EDGE_DEV = 1024
N_LAT = 8
N_LON = 32


def edge_lists(key):
    k_middle, k_polar, k_chosen, k_recv, k_block, k_rows = jax.random.split(key, 6)
    shape = (N_LAT, N_LON, EDGE_DEV)
    band_ids = jnp.arange(N_LAT, dtype=jnp.int32)[:, None]
    at_pole = (band_ids == 0) | (band_ids == N_LAT - 1)
    middle_load = jax.random.randint(k_middle, (N_LAT, N_LON), EDGE_DEV // 3, 2 * EDGE_DEV // 3 + 1)
    polar_load = jax.random.randint(k_polar, (N_LAT, N_LON), 3 * EDGE_DEV // 4, EDGE_DEV + 1)
    loads = jnp.where(at_pole, polar_load, middle_load)
    chosen = jax.random.randint(k_chosen, (), 0, N_LAT * N_LON)
    region_ids = jnp.arange(N_LAT * N_LON, dtype=jnp.int32).reshape(N_LAT, N_LON)
    loads = jnp.where(region_ids == chosen, EDGE_DEV, loads)
    slot_ids = jnp.arange(EDGE_DEV, dtype=jnp.int32)[None, None, :]
    filled = slot_ids < loads[:, :, None]
    recv_rows = jax.random.randint(k_recv, shape, 0, NODE_DEV)
    choose_block = jax.random.randint(k_block, shape, 0, 18)
    neighbours = jnp.array([0, 1, 2, 3, 5, 6, 7, 8], dtype=jnp.int32)
    block_ids = jnp.where(choose_block < 10, 4, neighbours[jnp.clip(choose_block - 10, 0, 7)])
    lat_grid = jnp.arange(N_LAT, dtype=jnp.int32)[:, None, None]
    block_ids = jnp.where((lat_grid == 0) & (block_ids < 3), 4, block_ids)
    block_ids = jnp.where((lat_grid == N_LAT - 1) & (block_ids > 5), 4, block_ids)
    row_ids = jax.random.randint(k_rows, shape, 0, NODE_DEV)
    sender_ids = jnp.where(filled, block_ids * NODE_DEV + row_ids, -1).astype(jnp.int32)
    receiver_ids = jnp.where(filled, recv_rows, -1).astype(jnp.int32)
    return (sender_ids, receiver_ids)


def draw_senders(key, part):
    return edge_lists(key)[0]


def draw_receivers(key, part):
    return edge_lists(key)[1]


def field_draw(key, base_scale, slope_sign):
    k_rows, k_cols, k_base = jax.random.split(key, 3)
    shape = (N_LAT, N_LON, NODE_DEV, LATENT)
    row_scale = jnp.exp(jax.random.uniform(k_rows, (N_LAT, N_LON, NODE_DEV, 1)) * math.log(10.0))
    col_scale = jnp.exp(jax.random.uniform(k_cols, (1, 1, 1, LATENT)) * math.log(10.0))
    lon_grid = jnp.arange(N_LON, dtype=jnp.float32)[None, :, None, None]
    lat_grid = jnp.arange(N_LAT, dtype=jnp.float32)[:, None, None, None]
    lon_place = 0.5 + slope_sign * (lon_grid / (N_LON - 1) - 0.5)
    lat_place = 0.5 + slope_sign * (lat_grid / (N_LAT - 1) - 0.5)
    device_scale = jnp.exp(lon_place * math.log(3.0) + lat_place * math.log(2.0))
    base = jax.random.normal(k_base, shape)
    base = jnp.clip(base, -4.0, 4.0)
    return (base * row_scale * col_scale * device_scale * base_scale).astype(jnp.float32)


def draw_residual(key, part):
    key = jax.random.fold_in(key, 11)
    return field_draw(key, 0.05, 1.0)


def draw_direction(key, part):
    key = jax.random.fold_in(key, 23)
    return field_draw(key, 0.05, -1.0)


def level_of(key, shape, shards, low, high):
    def one(axis_at, shards_of):
        heights = jax.random.uniform(jax.random.fold_in(jax.random.fold_in(key, 6), axis_at), (shards_of,), jnp.float32, low / len(shards), high / len(shards))
        return jnp.repeat(jnp.exp(heights), shape[axis_at] // shards_of).reshape((-1,) + (1,) * (len(shape) - axis_at - 1))

    factor_of = one(*shards[0])
    for cut in shards[1:]:
        factor_of = factor_of * one(*cut)
    return factor_of


def bell_draw(key, shape, width, reach, cuts=(), kind=jnp.bfloat16):
    drawn = jax.random.normal(key, shape, jnp.float32) * width
    if len(cuts) > 0:
        drawn = level_of(key, shape, cuts, -0.22, 0.18) * drawn
    return jnp.clip(drawn, min=-reach, max=reach).astype(kind)


def setup_inputs(seed: int = 0) -> dict:
    key_of = jax.random.split(jax.random.key(seed), 15)
    return {
        "x_field": bell_draw(key_of[0], (N_LAT, N_LON, NODE_DEV, LATENT), 1.0, 6.0, ((0, 8), (1, 32)), jnp.float32),
        "residual": draw_residual(jax.random.fold_in(key_of[14], 71), 0),
        "direction": draw_direction(jax.random.fold_in(key_of[14], 71), 0),
        "a_node": bell_draw(key_of[3], (N_LAT, N_LON, NODE_DEV, LATENT), 1.5, 6.0, ((0, 8), (1, 32))),
        "a_edge": bell_draw(key_of[4], (N_LAT, N_LON, EDGE_DEV, LATENT), 1.5, 6.0, ((0, 8), (1, 32))),
        "senders": draw_senders(jax.random.fold_in(key_of[14], 71), 0),
        "receivers": draw_receivers(jax.random.fold_in(key_of[14], 71), 0),
        "obs_weight": jnp.clip(jnp.exp(math.log(4.0) - 2.0794415 * jax.random.uniform(key_of[7], (N_LAT, N_LON, NODE_DEV), jnp.float32) ** level_of(key_of[7], (N_LAT, N_LON, NODE_DEV), ((0, 8), (1, 32)), -0.2, 0.2)), 0.5, 4.0),
        "w_send": bell_draw(key_of[8], (LATENT, LATENT), LATENT ** -0.5, 0.25),
        "w_recv": bell_draw(key_of[9], (LATENT, LATENT), LATENT ** -0.5, 0.25),
        "w_edge_out": bell_draw(key_of[10], (LATENT, LATENT), LATENT ** -0.5, 0.25),
        "w_node_self": bell_draw(key_of[11], (LATENT, LATENT), LATENT ** -0.5, 0.25),
        "w_node_msg": bell_draw(key_of[12], (LATENT, LATENT), LATENT ** -0.5, 0.25),
        "w_node_out": bell_draw(key_of[13], (LATENT, LATENT), LATENT ** -0.5, 0.25),
    }


def silu_slope(value):
    sigmoid_value = jax.nn.sigmoid(value)
    return sigmoid_value * (1.0 + value * (1.0 - sigmoid_value))


def dot_back(left, weight):
    return lax.dot_general(left, weight, (((1,), (1,)), ((), ())), preferred_element_type=jnp.float32)


def reference(x_field, residual, direction, a_node, a_edge, senders, receivers, obs_weight, w_send, w_recv, w_edge_out, w_node_self, w_node_msg, w_node_out):
    node_count = N_LAT * N_LON * NODE_DEV
    stripe_nodes = N_LON * NODE_DEV
    lat_ids = jnp.arange(N_LAT, dtype=jnp.int32)[:, None, None]
    lon_ids = jnp.arange(N_LON, dtype=jnp.int32)[None, :, None]
    filled = receivers >= 0
    safe_send = jnp.where(filled, senders, 0).astype(jnp.int32)
    block_ids = safe_send // NODE_DEV
    row_ids = safe_send % NODE_DEV
    send_lat = lat_ids + block_ids // 3 - 1
    send_lon = (lon_ids + block_ids % 3 - 1) % N_LON
    send_index = jnp.where(filled, (send_lat * N_LON + send_lon) * NODE_DEV + row_ids, 0).astype(jnp.int32)
    recv_index = jnp.where(filled, lon_ids * NODE_DEV + receivers, 0).astype(jnp.int32)
    filled_edges = filled.astype(jnp.float32)[..., None]

    search = direction.reshape(node_count, LATENT)
    search_bf = search.astype(jnp.bfloat16)
    send_term = jnp.dot(search_bf, w_send, preferred_element_type=jnp.float32).astype(jnp.bfloat16)
    recv_term = jnp.dot(search_bf, w_recv, preferred_element_type=jnp.float32).astype(jnp.bfloat16)
    recv_stripes = recv_term.reshape(N_LAT, stripe_nodes, LATENT)

    def tangent_stripe(stripe):
        sends = send_index[stripe].reshape(-1)
        recvs = recv_index[stripe].reshape(-1)
        weights = filled_edges[stripe].reshape(-1, 1)
        edge_act = a_edge[stripe].reshape(-1, LATENT).astype(jnp.float32)
        gathered = send_term[sends].astype(jnp.float32) + recv_stripes[stripe][recvs].astype(jnp.float32)
        hidden = (silu_slope(edge_act) * gathered).astype(jnp.bfloat16)
        message = jnp.dot(hidden, w_edge_out, preferred_element_type=jnp.float32).astype(jnp.bfloat16)
        return jax.ops.segment_sum(message.astype(jnp.float32) * weights, recvs, stripe_nodes)

    inbox = lax.map(tangent_stripe, jnp.arange(N_LAT, dtype=jnp.int32)).reshape(node_count, LATENT)
    node_slope = silu_slope(a_node.reshape(node_count, LATENT).astype(jnp.float32))
    pre_node = jnp.dot(search_bf, w_node_self, preferred_element_type=jnp.float32) + jnp.dot(inbox.astype(jnp.bfloat16), w_node_msg, preferred_element_type=jnp.float32)
    node_hidden = (node_slope * pre_node).astype(jnp.bfloat16)
    changed = search + jnp.dot(node_hidden, w_node_out, preferred_element_type=jnp.float32)
    observed = obs_weight.reshape(node_count, 1) * changed
    observed_bf = observed.astype(jnp.bfloat16)
    node_grad = (dot_back(observed_bf, w_node_out) * node_slope).astype(jnp.bfloat16)
    back_self = dot_back(node_grad, w_node_self)
    msg_grad = dot_back(node_grad, w_node_msg).astype(jnp.bfloat16)
    msg_stripes = msg_grad.reshape(N_LAT, stripe_nodes, LATENT)

    def adjoint_stripe(total, stripe):
        sends = send_index[stripe].reshape(-1)
        recvs = recv_index[stripe].reshape(-1)
        weights = filled_edges[stripe].reshape(-1, 1)
        edge_act = a_edge[stripe].reshape(-1, LATENT).astype(jnp.float32)
        edge_in = jnp.where(weights > 0, msg_stripes[stripe][recvs], jnp.zeros((), jnp.bfloat16))
        edge_grad = (dot_back(edge_in, w_edge_out) * silu_slope(edge_act)).astype(jnp.bfloat16)
        to_send = dot_back(edge_grad, w_send).astype(jnp.bfloat16)
        to_recv = dot_back(edge_grad, w_recv).astype(jnp.bfloat16)
        total = total + jax.ops.segment_sum(to_send.astype(jnp.float32) * weights, sends, node_count)
        return total, jax.ops.segment_sum(to_recv.astype(jnp.float32) * weights, recvs, stripe_nodes)

    back_send, back_recv = lax.scan(adjoint_stripe, jnp.zeros((node_count, LATENT), jnp.float32), jnp.arange(N_LAT, dtype=jnp.int32))
    back_recv = back_recv.reshape(node_count, LATENT)
    product = (search + observed + back_self + back_send + back_recv).reshape(direction.shape)

    norm_now = jnp.sum(residual * residual)
    curvature = jnp.sum(direction * product)
    alpha = norm_now / curvature
    new_field = x_field + alpha * direction
    new_residual = residual - alpha * product
    norm_next = jnp.sum(new_residual * new_residual)
    new_direction = new_residual + (norm_next / norm_now) * direction
    return (new_field, new_residual, new_direction)
```

```python
import jax
import jax.numpy as jnp
from jax import lax
from jax.experimental import pallas as pl
from jax.experimental.pallas import tpu as pltpu
from jax.sharding import PartitionSpec as P

BF = jnp.bfloat16
F32 = jnp.float32
ORDER = (0, 2, 6, 8, 1, 7, 3, 5, 4)
VMEM_LIMIT = 12 * 1024 * 1024


def dot(left, right):
    return jnp.dot(left, right, preferred_element_type=F32)


def dot_back(left, weight):
    return lax.dot_general(left, weight, (((1,), (1,)), ((), ())), preferred_element_type=F32)


def silu_slope(value):
    sig = 0.5 * jnp.tanh(0.5 * value) + 0.5
    return sig * (1.0 + value * (1.0 - sig))


def call(kernel, name, out_shape, *args):
    spec = pl.BlockSpec(memory_space=pltpu.VMEM)
    return pl.pallas_call(
        kernel,
        out_shape=out_shape,
        in_specs=[spec] * len(args),
        out_specs=jax.tree.map(lambda _: spec, out_shape),
        compiler_params=pltpu.CompilerParams(vmem_limit_bytes=VMEM_LIMIT),
        name=name,
    )(*args)


def shape(rows, cols, kind):
    return jax.ShapeDtypeStruct((rows, cols), kind)


def send_kernel(d_ref, w_ref, out_ref):
    out_ref[...] = dot(d_ref[...].astype(BF), w_ref[...]).astype(BF)


def pick_kernel(act, send_col, send_row, recv_col, recv_row, slope, pick, pick_t):
    edges = act.shape[0]
    nodes = 128
    slope[...] = silu_slope(act[...].astype(F32))
    lanes = lax.broadcasted_iota(jnp.int32, (edges, nodes), 1)
    rows = lax.broadcasted_iota(jnp.int32, (nodes, edges), 0)
    s_col = jnp.broadcast_to(send_col[...], (edges, nodes)) - lanes
    s_row = jnp.broadcast_to(send_row[...], (nodes, edges)) - rows
    for k, b in enumerate(ORDER):
        pick[:, k * nodes : (k + 1) * nodes] = jnp.where(s_col == b * nodes, 1.0, 0.0).astype(BF)
        pick_t[k * nodes : (k + 1) * nodes, :] = jnp.where(s_row == b * nodes, 1.0, 0.0).astype(BF)
    k = len(ORDER)
    r_col = jnp.broadcast_to(recv_col[...], (edges, nodes))
    r_row = jnp.broadcast_to(recv_row[...], (nodes, edges))
    pick[:, k * nodes :] = jnp.where(r_col == lanes, 1.0, 0.0).astype(BF)
    pick_t[k * nodes :, :] = jnp.where(r_row == rows, 1.0, 0.0).astype(BF)


def base_kernel(
    d, own, north, south, west, east, pick, a_node, w_recv, w_self, w_edge, w_msg,
    base, node_slope, self_pre, fold, table,
):
    d_bf = d[...].astype(BF)
    for k, part in enumerate((north, south, west, east, own)):
        table[k * 128 : (k + 1) * 128, :] = part[...]
    table[5 * 128 :, :] = dot(d_bf, w_recv[...]).astype(BF)
    base[...] = dot(pick[:, 512:], table[...])
    node_slope[...] = silu_slope(a_node[...].astype(F32))
    self_pre[...] = dot(d_bf, w_self[...])
    fold[...] = dot(w_edge[...], w_msg[...]).astype(BF)


def main_kernel(
    nw, ne, sw, se, base, slope, pick, pick_t, d, node_slope, self_pre, fold, w_out, obs,
    to_north, to_south, edge_grad, node_grad, observed, table,
):
    for k, part in enumerate((nw, ne, sw, se)):
        table[k * 128 : (k + 1) * 128, :] = part[...]
    gathered = base[...] + dot(pick[:, :512], table[...])
    hidden = (slope[...] * gathered).astype(BF)
    hidden_sum = dot(pick_t[1152:, :], hidden).astype(BF)
    pre_node = self_pre[...] + dot(hidden_sum, fold[...])
    node_hidden = (node_slope[...] * pre_node).astype(BF)
    changed = d[...] + dot(node_hidden, w_out[...])
    seen = obs[...] * changed
    observed[...] = seen
    grad = (dot_back(seen.astype(BF), w_out[...]) * node_slope[...]).astype(BF)
    node_grad[...] = grad
    edge_back = dot_back(grad, fold[...]).astype(BF)
    e_grad = (dot(pick[:, 1152:], edge_back) * slope[...]).astype(BF)
    edge_grad[...] = e_grad
    sums = dot(pick_t[:768, :], e_grad).astype(BF)
    to_north[0:128, :] = sums[0:128, :]
    to_north[128:256, :] = sums[512:640, :]
    to_north[256:384, :] = sums[128:256, :]
    to_south[0:128, :] = sums[256:384, :]
    to_south[128:256, :] = sums[640:768, :]
    to_south[256:384, :] = sums[384:512, :]


def rest_kernel(edge_grad, pick_t, node_grad, observed, d, w_recv, w_self, mid, partial):
    sums = dot(pick_t[768:, :], edge_grad[...])
    mid[...] = sums[:384, :]
    back = dot_back(node_grad[...], w_self[...]) + dot_back(sums[384:, :].astype(BF), w_recv[...])
    partial[...] = d[...] + observed[...] + back


def merge_kernel(mid, from_north, from_south, to_west, to_east, center):
    def both(rows):
        return from_north[rows, :].astype(F32) + from_south[rows, :].astype(F32)

    to_west[...] = (mid[0:128, :] + both(pl.ds(0, 128))).astype(BF)
    to_east[...] = (mid[128:256, :] + both(pl.ds(256, 128))).astype(BF)
    center[...] = mid[256:384, :] + both(pl.ds(128, 128))


def product_kernel(center, from_west, from_east, partial, w_send, d, r, product, sums):
    total = center[...] + from_west[...].astype(F32) + from_east[...].astype(F32)
    prod = partial[...] + dot_back(total.astype(BF), w_send[...])
    product[...] = prod
    res = r[...]
    lane = lax.broadcasted_iota(jnp.int32, sums.shape, 1)
    out = jnp.zeros(sums.shape, F32)
    for k, value in enumerate((res * res, d[...] * prod, res * prod, prod * prod)):
        out = jnp.where(lane == k, jnp.sum(value), out)
    sums[...] = out


def final_kernel(sums, x, r, d, product, new_x, new_r, new_d):
    total = jnp.sum(sums[...], axis=0, keepdims=True)
    norm_now, curvature = total[:, 0:1], total[:, 1:2]
    cross, square = total[:, 2:3], total[:, 3:4]
    alpha = norm_now / curvature
    norm_next = jnp.maximum(norm_now + alpha * (alpha * square - 2.0 * cross), 0.0)
    beta = norm_next / norm_now
    search = d[...]
    new_x[...] = x[...] + alpha * search
    left = r[...] - alpha * product[...]
    new_r[...] = left
    new_d[...] = left + beta * search


def shifted(value, axis, step):
    count = lax.axis_size(axis)
    return lax.ppermute(value, axis, [(i, (i + step) % count) for i in range(count)])


def total_rows(value, axis):
    return lax.all_to_all(value, axis, 0, 0, tiled=True)


def body(
    x_field, residual, direction, a_node, a_edge, senders, receivers, obs_weight,
    w_send, w_recv, w_edge_out, w_node_self, w_node_msg, w_node_out,
):
    nodes, width = x_field.shape[2:]
    edges = a_edge.shape[2]
    x = x_field.reshape(nodes, width)
    r = residual.reshape(nodes, width)
    d = direction.reshape(nodes, width)
    own = call(send_kernel, "send_term", shape(nodes, width, BF), d, w_send)
    west = shifted(own, "lon", 1)
    east = shifted(own, "lon", -1)
    north = shifted(own, "lat", 1)
    south = shifted(own, "lat", -1)
    slope, pick, pick_t = call(
        pick_kernel,
        "pickers",
        (shape(edges, width, F32), shape(edges, 10 * nodes, BF), shape(10 * nodes, edges, BF)),
        a_edge.reshape(edges, width),
        senders.reshape(edges, 1),
        senders.reshape(1, edges),
        receivers.reshape(edges, 1),
        receivers.reshape(1, edges),
    )
    nw = shifted(west, "lat", 1)
    ne = shifted(east, "lat", 1)
    sw = shifted(west, "lat", -1)
    se = shifted(east, "lat", -1)

    spec = pl.BlockSpec(memory_space=pltpu.VMEM)
    params = pltpu.CompilerParams(vmem_limit_bytes=VMEM_LIMIT)
    base, node_slope, self_pre, fold = pl.pallas_call(
        base_kernel,
        out_shape=(
            shape(edges, width, F32),
            shape(nodes, width, F32),
            shape(nodes, width, F32),
            shape(width, width, BF),
        ),
        in_specs=[spec] * 12,
        out_specs=(spec,) * 4,
        scratch_shapes=[pltpu.VMEM((6 * nodes, width), BF)],
        compiler_params=params,
        name="base",
    )(
        d, own, north, south, west, east, pick, a_node.reshape(nodes, width),
        w_recv, w_node_self, w_edge_out, w_node_msg,
    )
    to_north, to_south, edge_grad, node_grad, observed = pl.pallas_call(
        main_kernel,
        out_shape=(
            shape(3 * nodes, width, BF),
            shape(3 * nodes, width, BF),
            shape(edges, width, BF),
            shape(nodes, width, BF),
            shape(nodes, width, F32),
        ),
        in_specs=[spec] * 14,
        out_specs=(spec,) * 5,
        scratch_shapes=[pltpu.VMEM((4 * nodes, width), BF)],
        compiler_params=params,
        name="main",
    )(
        nw, ne, sw, se, base, slope, pick, pick_t, d, node_slope, self_pre, fold, w_node_out,
        obs_weight.reshape(nodes, 1),
    )
    from_south = shifted(to_north, "lat", -1)
    from_north = shifted(to_south, "lat", 1)
    mid, partial = call(
        rest_kernel,
        "rest",
        (shape(3 * nodes, width, F32), shape(nodes, width, F32)),
        edge_grad, pick_t, node_grad, observed, d, w_recv, w_node_self,
    )
    to_west, to_east, center = call(
        merge_kernel,
        "merge",
        (shape(nodes, width, BF), shape(nodes, width, BF), shape(nodes, width, F32)),
        mid, from_north, from_south,
    )
    from_east = shifted(to_west, "lon", -1)
    from_west = shifted(to_east, "lon", 1)
    n_lat, n_lon = lax.axis_size("lat"), lax.axis_size("lon")
    product, sums = call(
        product_kernel,
        "product",
        (shape(nodes, width, F32), shape(n_lat, 128, F32)),
        center, from_west, from_east, partial, w_send, d, r,
    )
    band = jnp.sum(total_rows(sums, "lat"), axis=0, keepdims=True)
    every = total_rows(jnp.broadcast_to(band, (n_lon, 128)), "lon")
    outs = call(
        final_kernel, "final", (shape(nodes, width, F32),) * 3, every, x, r, d, product
    )
    return tuple(out.reshape(x_field.shape) for out in outs)


def solution(mesh):
    field = P("lat", "lon", None, None)
    flat = P("lat", "lon", None)
    return jax.shard_map(
        body,
        mesh=mesh,
        in_specs=(field,) * 5 + (flat,) * 3 + (P(),) * 6,
        out_specs=(field,) * 3,
        check_vma=False,
    )
```

```python
import jax
import jax.numpy as jnp
from jax import lax
from jax.experimental import pallas as pl
from jax.experimental.pallas import tpu as pltpu
from jax.sharding import PartitionSpec as P

BF = jnp.bfloat16
F32 = jnp.float32
ORDER = (0, 2, 6, 8, 1, 7, 3, 5, 4)
VMEM_LIMIT = 12 * 1024 * 1024


def dot(left, right):
    return jnp.dot(left, right, preferred_element_type=F32)


def dot_back(left, weight):
    return lax.dot_general(left, weight, (((1,), (1,)), ((), ())), preferred_element_type=F32)


def silu_slope(value):
    sig = 0.5 * jnp.tanh(0.5 * value) + 0.5
    return sig * (1.0 + value * (1.0 - sig))


def call(kernel, name, out_shape, args, scratch=(), hbm=False):
    here = pl.BlockSpec(memory_space=pltpu.VMEM)
    there = pl.BlockSpec(memory_space=pltpu.HBM)
    if hbm:
        args = [pltpu.with_memory_space_constraint(arg, pltpu.HBM) for arg in args]
    return pl.pallas_call(
        kernel,
        out_shape=out_shape,
        in_specs=[there if hbm else here] * len(args),
        out_specs=jax.tree.map(lambda _: here, out_shape),
        scratch_shapes=scratch,
        compiler_params=pltpu.CompilerParams(vmem_limit_bytes=VMEM_LIMIT),
        name=name,
    )(*args)


def shape(rows, cols, kind):
    return jax.ShapeDtypeStruct((rows, cols), kind)


def send_kernel(d_hbm, w_hbm, out_ref, d, w, sems):
    copies = [pltpu.make_async_copy(d_hbm, d, sems.at[0]), pltpu.make_async_copy(w_hbm, w, sems.at[1])]
    for copy in copies:
        copy.start()
    for copy in copies:
        copy.wait()
    out_ref[...] = dot(d[...].astype(BF), w[...]).astype(BF)


def prepare_kernel(
    senders, receivers, act, d_hbm, a_node_hbm, w_recv_hbm, w_self_hbm, w_edge_hbm, w_msg_hbm, w_out_hbm,
    slope, pick, pick_t, d, a_node, w_recv, w_self, w_edge, w_msg, w_out,
    send_row, recv_row, act_here, sems,
):
    pairs = (
        (senders, send_row), (receivers, recv_row), (act, act_here), (d_hbm, d), (a_node_hbm, a_node),
        (w_recv_hbm, w_recv), (w_self_hbm, w_self), (w_edge_hbm, w_edge), (w_msg_hbm, w_msg), (w_out_hbm, w_out),
    )
    copies = [pltpu.make_async_copy(a, b, sems.at[k]) for k, (a, b) in enumerate(pairs)]
    for copy in copies:
        copy.start()
    edges = act_here.shape[0]
    nodes = 128
    copies[0].wait()
    copies[1].wait()
    rows = lax.broadcasted_iota(jnp.int32, (nodes, edges), 0)
    lanes = lax.broadcasted_iota(jnp.int32, (edges, nodes), 1)
    sends = jnp.broadcast_to(send_row[...], (nodes, edges))
    recvs = jnp.broadcast_to(recv_row[...], (nodes, edges))
    s_row = sends - rows
    s_col = jnp.transpose(sends) - lanes
    r_col = jnp.transpose(recvs)
    for k, b in enumerate(ORDER):
        pick[:, k * nodes : (k + 1) * nodes] = jnp.where(s_col == b * nodes, 1.0, 0.0).astype(BF)
        pick_t[k * nodes : (k + 1) * nodes, :] = jnp.where(s_row == b * nodes, 1.0, 0.0).astype(BF)
    k = len(ORDER)
    pick[:, k * nodes :] = jnp.where(r_col == lanes, 1.0, 0.0).astype(BF)
    pick_t[k * nodes :, :] = jnp.where(recvs == rows, 1.0, 0.0).astype(BF)
    copies[2].wait()
    slope[...] = silu_slope(act_here[...].astype(F32))
    for copy in copies[3:]:
        copy.wait()


def stack_kernel(north, south, west, east, after, out):
    out[0:128, :] = west[...]
    out[128:256, :] = east[...]


def base_kernel(
    d, own, north, south, west, east, pick, a_node, w_recv, w_self, w_edge, w_msg, w_out,
    base, node_slope, self_pre, fold, gram, d_back, table,
):
    d_bf = d[...].astype(BF)
    for k, part in enumerate((north, south, west, east, own)):
        table[k * 128 : (k + 1) * 128, :] = part[...]
    table[5 * 128 :, :] = dot(d_bf, w_recv[...]).astype(BF)
    base[...] = dot(pick[:, 512:], table[...])
    node_slope[...] = silu_slope(a_node[...].astype(F32))
    self_pre[...] = dot(d_bf, w_self[...])
    fold[...] = dot(w_edge[...], w_msg[...]).astype(BF)
    gram[...] = dot_back(w_out[...], w_out[...]).astype(BF)
    d_back[...] = dot_back(d_bf, w_out[...])


def lanes_of(row, width):
    nodes = row.shape[1]
    column = jnp.transpose(jnp.broadcast_to(row, (nodes, nodes)))
    return jnp.concatenate([column] * (width // nodes), axis=1)


def main_kernel(
    from_n, from_s, base, slope, pick, pick_t, node_slope, self_pre, fold, gram, d_back, obs,
    corner_n, corner_s, edge_grad, node_grad, node_hidden, table,
):
    table[0:256, :] = from_n[...]
    table[256:512, :] = from_s[...]
    gathered = base[...] + dot(pick[:, :512], table[...])
    hidden = (slope[...] * gathered).astype(BF)
    hidden_sum = dot(pick_t[1152:, :], hidden).astype(BF)
    pre_node = self_pre[...] + dot(hidden_sum, fold[...])
    inner = (node_slope[...] * pre_node).astype(BF)
    node_hidden[...] = inner
    back = lanes_of(obs[...], inner.shape[1]) * (d_back[...] + dot(inner, gram[...]))
    grad = (back * node_slope[...]).astype(BF)
    node_grad[...] = grad
    edge_back = dot_back(grad, fold[...]).astype(BF)
    e_grad = (dot(pick[:, 1152:], edge_back) * slope[...]).astype(BF)
    edge_grad[...] = e_grad
    corner_n[...] = dot(pick_t[0:256, :], e_grad).astype(BF)
    corner_s[...] = dot(pick_t[256:512, :], e_grad).astype(BF)


def rest_kernel(
    edge_grad, pick_t, node_grad, node_hidden, obs, d, w_recv, w_self, w_out,
    middle_n, middle_s, mid, partial,
):
    sums = dot(pick_t[512:, :], edge_grad[...])
    middle_n[...] = sums[:128, :].astype(BF)
    middle_s[...] = sums[128:256, :].astype(BF)
    mid[...] = sums[256:640, :]
    search = d[...]
    changed = search + dot(node_hidden[...], w_out[...])
    observed = lanes_of(obs[...], search.shape[1]) * changed
    back = dot_back(node_grad[...], w_self[...]) + dot_back(sums[640:, :].astype(BF), w_recv[...])
    partial[...] = search + observed + back


def merge_kernel(mid, from_n, from_s, to_west, to_east):
    west, east = slice(0, 128), slice(128, 256)
    for side, out in ((west, to_west), (east, to_east)):
        out[...] = (mid[side, :] + from_n[side, :].astype(F32) + from_s[side, :].astype(F32)).astype(BF)


def product_kernel(
    mid, from_n, from_s, from_w, from_e, partial, w_send, d, r, product, sums
):
    total = mid[256:384, :]
    for part in (from_n, from_s, from_w, from_e):
        total = total + part[...].astype(F32)
    prod = partial[...] + dot_back(total.astype(BF), w_send[...])
    product[...] = prod
    res = r[...]
    lane = lax.broadcasted_iota(jnp.int32, sums.shape, 1)
    out = jnp.zeros(sums.shape, F32)
    for k, value in enumerate((res * res, d[...] * prod, res * prod, prod * prod)):
        out = jnp.where(lane == k, jnp.sum(value), out)
    sums[...] = out


def final_kernel(sums, x, r, d, product, new_x, new_r, new_d):
    total = jnp.sum(sums[...], axis=0, keepdims=True)
    norm_now, curvature = total[:, 0:1], total[:, 1:2]
    cross, square = total[:, 2:3], total[:, 3:4]
    alpha = norm_now / curvature
    norm_next = jnp.maximum(norm_now + alpha * (alpha * square - 2.0 * cross), 0.0)
    beta = norm_next / norm_now
    search = d[...]
    new_x[...] = x[...] + alpha * search
    left = r[...] - alpha * product[...]
    new_r[...] = left
    new_d[...] = left + beta * search


def shifted(value, axis, step):
    count = lax.axis_size(axis)
    return lax.ppermute(value, axis, [(i, (i + step) % count) for i in range(count)])


def sums_everywhere(value):
    n_lat, n_lon = lax.axis_size("lat"), lax.axis_size("lon")
    near = n_lon // 4
    first = [
        [(2 * y + c) * n_lon + x * near + z for c in range(2) for z in range(near)]
        for y in range(n_lat // 2)
        for x in range(4)
    ]
    second = [
        [(2 * y + c) * n_lon + x * near + z for y in range(n_lat // 2) for x in range(4)]
        for c in range(2)
        for z in range(near)
    ]
    value = lax.all_to_all(value, ("lat", "lon"), 0, 0, tiled=True, axis_index_groups=first)
    value = jnp.sum(value, axis=0, keepdims=True)
    value = jnp.broadcast_to(value, (len(second[0]), value.shape[1]))
    return lax.all_to_all(value, ("lat", "lon"), 0, 0, tiled=True, axis_index_groups=second)


def body(
    x_field, residual, direction, a_node, a_edge, senders, receivers, obs_weight,
    w_send, w_recv, w_edge_out, w_node_self, w_node_msg, w_node_out,
):
    nodes, width = x_field.shape[2:]
    edges = a_edge.shape[2]
    x = x_field.reshape(nodes, width)
    r = residual.reshape(nodes, width)
    d_hbm = direction.reshape(nodes, width)
    obs = obs_weight.reshape(1, nodes)
    field = shape(nodes, width, F32)
    block = shape(nodes, width, BF)
    weight = shape(width, width, BF)
    own = call(
        send_kernel, "send_term", block, (d_hbm, w_send), hbm=True,
        scratch=(pltpu.VMEM((nodes, width), F32), pltpu.VMEM((width, width), BF), pltpu.SemaphoreType.DMA((2,))),
    )
    north = shifted(own, "lat", 1)
    south = shifted(own, "lat", -1)
    west = shifted(own, "lon", 1)
    east = shifted(own, "lon", -1)
    slope, pick, pick_t, d, node_act, w_recv, w_self, w_edge, w_msg, w_out = call(
        prepare_kernel,
        "prepare",
        (
            shape(edges, width, F32),
            shape(edges, 10 * nodes, BF),
            shape(10 * nodes, edges, BF),
            field,
            block,
        )
        + (weight,) * 5,
        (
            senders.reshape(1, edges), receivers.reshape(1, edges), a_edge.reshape(edges, width), d_hbm,
            a_node.reshape(nodes, width), w_recv, w_node_self, w_edge_out, w_node_msg, w_node_out,
        ),
        hbm=True,
        scratch=(
            pltpu.VMEM((1, edges), jnp.int32),
            pltpu.VMEM((1, edges), jnp.int32),
            pltpu.VMEM((edges, width), BF),
            pltpu.SemaphoreType.DMA((10,)),
        ),
    )
    beside = call(stack_kernel, "stack", shape(2 * nodes, width, BF), (north, south, west, east, node_act))
    from_n = shifted(beside, "lat", 1)
    from_s = shifted(beside, "lat", -1)
    base, node_slope, self_pre, fold, gram, d_back = call(
        base_kernel,
        "base",
        (shape(edges, width, F32), field, field, weight, weight, field),
        (d, own, north, south, west, east, pick, node_act, w_recv, w_self, w_edge, w_msg, w_out),
        scratch=(pltpu.VMEM((6 * nodes, width), BF),),
    )
    corner_n, corner_s, edge_grad, node_grad, node_hidden = call(
        main_kernel,
        "main",
        (shape(2 * nodes, width, BF),) * 2 + (shape(edges, width, BF), block, block),
        (from_n, from_s, base, slope, pick, pick_t, node_slope, self_pre, fold, gram, d_back, obs),
        scratch=(pltpu.VMEM((4 * nodes, width), BF),),
    )
    from_s = shifted(corner_n, "lat", -1)
    from_n = shifted(corner_s, "lat", 1)
    middle_n, middle_s, mid, partial = call(
        rest_kernel,
        "rest",
        (block, block, shape(3 * nodes, width, F32), field),
        (edge_grad, pick_t, node_grad, node_hidden, obs, d, w_recv, w_self, w_out),
    )
    to_west, to_east = call(merge_kernel, "merge", (block,) * 2, (mid, from_n, from_s))
    from_e = shifted(to_west, "lon", -1)
    from_w = shifted(to_east, "lon", 1)
    from_s = shifted(middle_n, "lat", -1)
    from_n = shifted(middle_s, "lat", 1)
    product, sums = call(
        product_kernel,
        "product",
        (field, shape(16, 128, F32)),
        (mid, from_n, from_s, from_w, from_e, partial, w_send, d, r),
    )
    sums = sums_everywhere(sums)
    outs = call(final_kernel, "final", (field,) * 3, (sums, x, r, d, product))
    return tuple(out.reshape(x_field.shape) for out in outs)


def solution(mesh):
    field = P("lat", "lon", None, None)
    flat = P("lat", "lon", None)
    return jax.shard_map(
        body,
        mesh=mesh,
        in_specs=(field,) * 5 + (flat,) * 3 + (P(),) * 6,
        out_specs=(field,) * 3,
        check_vma=False,
    )
```

```python
import jax
import jax.numpy as jnp
from jax import lax
from jax.experimental import pallas as pl
from jax.experimental.pallas import tpu as pltpu
from jax.sharding import PartitionSpec as P

BF = jnp.bfloat16
F32 = jnp.float32
VMEM_LIMIT = 12 * 1024 * 1024


def dot(left, right):
    return jnp.dot(left, right, preferred_element_type=F32)


def dot_back(left, weight):
    return lax.dot_general(left, weight, (((1,), (1,)), ((), ())), preferred_element_type=F32)


def silu_slope(value):
    sig = 0.5 * jnp.tanh(0.5 * value) + 0.5
    return sig * (1.0 + value * (1.0 - sig))


def call(kernel, name, out_shape, args, scratch=(), hbm=None):
    here = pl.BlockSpec(memory_space=pltpu.VMEM)
    there = pl.BlockSpec(memory_space=pltpu.HBM)
    first = len(args) if hbm is None else hbm
    away = [pltpu.with_memory_space_constraint(arg, pltpu.HBM) for arg in args[first:]]
    return pl.pallas_call(
        kernel,
        out_shape=out_shape,
        in_specs=[here] * first + [there] * len(away),
        out_specs=jax.tree.map(lambda _: here, out_shape),
        scratch_shapes=scratch,
        compiler_params=pltpu.CompilerParams(vmem_limit_bytes=VMEM_LIMIT),
        name=name,
    )(*args[:first], *away)


def shape(rows, cols, kind):
    return jax.ShapeDtypeStruct((rows, cols), kind)


def start_all(pairs, sems):
    copies = [pltpu.make_async_copy(a, b, sems.at[k]) for k, (a, b) in enumerate(pairs)]
    for copy in copies:
        copy.start()
    return copies


def slot_blocks():
    near = 6 - 6 * lax.rem(lax.axis_index("lat"), 2)
    far = 6 - near
    return (near, near + 2, far, far + 2, near + 1, far + 1, 3, 5, 4)


def send_kernel(senders, receivers, obs_hbm, d_hbm, w_hbm, own, send_row, recv_row, obs, d, w, sems):
    pairs = ((d_hbm, d), (w_hbm, w), (senders, send_row), (receivers, recv_row), (obs_hbm, obs))
    for copy in start_all(pairs, sems):
        copy.wait()
    own[...] = dot(d[...].astype(BF), w[...]).astype(BF)


def prepare_kernel(
    send_row, recv_row, act_hbm, a_node_hbm, w_recv_hbm, w_self_hbm, w_edge_hbm, w_msg_hbm, w_out_hbm,
    pick, pick_t, act, a_node, w_recv, w_self, w_edge, w_msg, w_out, sems,
):
    pairs = (
        (act_hbm, act), (a_node_hbm, a_node), (w_recv_hbm, w_recv), (w_self_hbm, w_self),
        (w_edge_hbm, w_edge), (w_msg_hbm, w_msg), (w_out_hbm, w_out),
    )
    copies = start_all(pairs, sems)
    edges = act.shape[0]
    nodes = 128
    rows = lax.broadcasted_iota(jnp.int32, (nodes, edges), 0)
    lanes = lax.broadcasted_iota(jnp.int32, (edges, nodes), 1)
    sends = jnp.broadcast_to(send_row[...], (nodes, edges))
    recvs = jnp.broadcast_to(recv_row[...], (nodes, edges))
    s_row = sends - rows
    s_col = jnp.transpose(sends) - lanes
    r_col = jnp.transpose(recvs)
    blocks = slot_blocks()
    for k, b in enumerate(blocks):
        pick[:, k * nodes : (k + 1) * nodes] = jnp.where(s_col == b * nodes, 1.0, 0.0).astype(BF)
        pick_t[k * nodes : (k + 1) * nodes, :] = jnp.where(s_row == b * nodes, 1.0, 0.0).astype(BF)
    k = len(blocks)
    pick[:, k * nodes :] = jnp.where(r_col == lanes, 1.0, 0.0).astype(BF)
    pick_t[k * nodes :, :] = jnp.where(recvs == rows, 1.0, 0.0).astype(BF)
    for copy in copies:
        copy.wait()


def stack_kernel(west, east, near, far, after, beside, across):
    beside[0:128, :] = west[...]
    beside[128:256, :] = east[...]
    across[0:128, :] = near[...]
    across[128:256, :] = far[...]


def base_kernel(
    d, own, across, beside, pick, act, a_node, w_recv, w_self, w_edge, w_msg, w_out,
    base, slope, node_slope, self_pre, fold, gram, d_back, table,
):
    d_bf = d[...].astype(BF)
    table[0:128, :] = own[...]
    table[128:256, :] = dot(d_bf, w_recv[...]).astype(BF)
    base[...] = (
        dot(pick[:, 512:768], across[...])
        + dot(pick[:, 768:1024], beside[...])
        + dot(pick[:, 1024:1280], table[...])
    )
    slope[...] = silu_slope(act[...].astype(F32))
    node_slope[...] = silu_slope(a_node[...].astype(F32))
    self_pre[...] = dot(d_bf, w_self[...])
    fold[...] = dot(w_edge[...], w_msg[...]).astype(BF)
    gram[...] = dot_back(w_out[...], w_out[...]).astype(BF)
    d_back[...] = dot_back(d_bf, w_out[...])


def lanes_of(row, width):
    nodes = row.shape[1]
    column = jnp.transpose(jnp.broadcast_to(row, (nodes, nodes)))
    return jnp.concatenate([column] * (width // nodes), axis=1)


def main_kernel(
    from_near, from_far, base, slope, pick, pick_t, node_slope, self_pre, fold, gram, d_back, obs,
    corner_near, corner_far, edge_grad, node_grad, node_hidden,
):
    gathered = (
        base[...] + dot(pick[:, 0:256], from_near[...]) + dot(pick[:, 256:512], from_far[...])
    )
    hidden = (slope[...] * gathered).astype(BF)
    hidden_sum = dot(pick_t[1152:, :], hidden).astype(BF)
    pre_node = self_pre[...] + dot(hidden_sum, fold[...])
    inner = (node_slope[...] * pre_node).astype(BF)
    node_hidden[...] = inner
    back = lanes_of(obs[...], inner.shape[1]) * (d_back[...] + dot(inner, gram[...]))
    grad = (back * node_slope[...]).astype(BF)
    node_grad[...] = grad
    edge_back = dot_back(grad, fold[...]).astype(BF)
    e_grad = (dot(pick[:, 1152:], edge_back) * slope[...]).astype(BF)
    edge_grad[...] = e_grad
    corner_near[...] = dot(pick_t[0:256, :], e_grad).astype(BF)
    corner_far[...] = dot(pick_t[256:512, :], e_grad).astype(BF)


def rest_kernel(
    edge_grad, pick_t, node_grad, node_hidden, obs, d, w_recv, w_self, w_out,
    middle_near, middle_far, mid, partial,
):
    sums = dot(pick_t[512:, :], edge_grad[...])
    middle_near[...] = sums[:128, :].astype(BF)
    middle_far[...] = sums[128:256, :].astype(BF)
    mid[...] = sums[256:640, :]
    search = d[...]
    changed = search + dot(node_hidden[...], w_out[...])
    observed = lanes_of(obs[...], search.shape[1]) * changed
    back = dot_back(node_grad[...], w_self[...]) + dot_back(sums[640:, :].astype(BF), w_recv[...])
    partial[...] = search + observed + back


def merge_kernel(mid, from_near, from_far, to_west, to_east):
    west, east = slice(0, 128), slice(128, 256)
    for side, out in ((west, to_west), (east, to_east)):
        out[...] = (
            mid[side, :] + from_near[side, :].astype(F32) + from_far[side, :].astype(F32)
        ).astype(BF)


def product_kernel(
    mid, from_near, from_far, from_w, from_e, partial, w_send, d, r, product, sums
):
    total = mid[256:384, :]
    for part in (from_near, from_far, from_w, from_e):
        total = total + part[...].astype(F32)
    prod = partial[...] + dot_back(total.astype(BF), w_send[...])
    product[...] = prod
    res = r[...]
    lane = lax.broadcasted_iota(jnp.int32, sums.shape, 1)
    out = jnp.zeros(sums.shape, F32)
    for k, value in enumerate((res * res, d[...] * prod, res * prod, prod * prod)):
        out = jnp.where(lane == k, jnp.sum(value), out)
    sums[...] = out


def final_kernel(sums, x, r, d, product, new_x, new_r, new_d):
    total = jnp.sum(sums[...], axis=0, keepdims=True)
    norm_now, curvature = total[:, 0:1], total[:, 1:2]
    cross, square = total[:, 2:3], total[:, 3:4]
    alpha = norm_now / curvature
    norm_next = jnp.maximum(norm_now + alpha * (alpha * square - 2.0 * cross), 0.0)
    beta = norm_next / norm_now
    search = d[...]
    new_x[...] = x[...] + alpha * search
    left = r[...] - alpha * product[...]
    new_r[...] = left
    new_d[...] = left + beta * search


def shifted(value, axis, step):
    count = lax.axis_size(axis)
    return lax.ppermute(value, axis, [(i, (i + step) % count) for i in range(count)])


def swapped(value, far):
    count = lax.axis_size("lat")
    step = -1 if far else 1
    pairs = [(i, (i + (step if i % 2 == 0 else -step)) % count) for i in range(count)]
    return lax.ppermute(value, "lat", pairs)


def sums_everywhere(value):
    n_lat, n_lon = lax.axis_size("lat"), lax.axis_size("lon")
    near = n_lon // 4
    first = [
        [(2 * y + c) * n_lon + x * near + z for c in range(2) for z in range(near)]
        for y in range(n_lat // 2)
        for x in range(4)
    ]
    second = [
        [(2 * y + c) * n_lon + x * near + z for y in range(n_lat // 2) for x in range(4)]
        for c in range(2)
        for z in range(near)
    ]
    value = lax.all_to_all(value, ("lat", "lon"), 0, 0, tiled=True, axis_index_groups=first)
    value = jnp.sum(value, axis=0, keepdims=True)
    value = jnp.broadcast_to(value, (len(second[0]), value.shape[1]))
    return lax.all_to_all(value, ("lat", "lon"), 0, 0, tiled=True, axis_index_groups=second)


def body(
    x_field, residual, direction, a_node, a_edge, senders, receivers, obs_weight,
    w_send, w_recv, w_edge_out, w_node_self, w_node_msg, w_node_out,
):
    nodes, width = x_field.shape[2:]
    edges = a_edge.shape[2]
    x = x_field.reshape(nodes, width)
    r = residual.reshape(nodes, width)
    d_hbm = direction.reshape(nodes, width)
    field = shape(nodes, width, F32)
    block = shape(nodes, width, BF)
    weight = shape(width, width, BF)
    own, send_row, recv_row, obs, d = call(
        send_kernel,
        "send_term",
        (
            block,
            shape(1, edges, jnp.int32),
            shape(1, edges, jnp.int32),
            shape(1, nodes, F32),
            field,
        ),
        (senders.reshape(1, edges), receivers.reshape(1, edges), obs_weight.reshape(1, nodes), d_hbm, w_send),
        hbm=0,
        scratch=(pltpu.VMEM((width, width), BF), pltpu.SemaphoreType.DMA((5,))),
    )
    near = swapped(own, False)
    far = swapped(own, True)
    west = shifted(own, "lon", 1)
    east = shifted(own, "lon", -1)
    pick, pick_t, act, node_act, w_recv, w_self, w_edge, w_msg, w_out = call(
        prepare_kernel,
        "prepare",
        (
            shape(edges, 10 * nodes, BF),
            shape(10 * nodes, edges, BF),
            shape(edges, width, BF),
            block,
        )
        + (weight,) * 5,
        (
            send_row, recv_row, a_edge.reshape(edges, width), a_node.reshape(nodes, width),
            w_recv, w_node_self, w_edge_out, w_node_msg, w_node_out,
        ),
        hbm=2,
        scratch=(pltpu.SemaphoreType.DMA((7,)),),
    )
    pair = shape(2 * nodes, width, BF)
    beside, across = call(stack_kernel, "stack", (pair, pair), (west, east, near, far, node_act))
    from_near = swapped(beside, False)
    from_far = swapped(beside, True)
    base, slope, node_slope, self_pre, fold, gram, d_back = call(
        base_kernel,
        "base",
        (shape(edges, width, F32),) * 2 + (field, field, weight, weight, field),
        (d, own, across, beside, pick, act, node_act, w_recv, w_self, w_edge, w_msg, w_out),
        scratch=(pltpu.VMEM((2 * nodes, width), BF),),
    )
    corner_near, corner_far, edge_grad, node_grad, node_hidden = call(
        main_kernel,
        "main",
        (pair, pair, shape(edges, width, BF), block, block),
        (
            from_near, from_far, base, slope, pick, pick_t, node_slope, self_pre, fold, gram, d_back, obs,
        ),
    )
    from_near = swapped(corner_near, False)
    from_far = swapped(corner_far, True)
    middle_near, middle_far, mid, partial = call(
        rest_kernel,
        "rest",
        (block, block, shape(3 * nodes, width, F32), field),
        (edge_grad, pick_t, node_grad, node_hidden, obs, d, w_recv, w_self, w_out),
    )
    to_west, to_east = call(merge_kernel, "merge", (block, block), (mid, from_near, from_far))
    from_e = shifted(to_west, "lon", -1)
    from_w = shifted(to_east, "lon", 1)
    from_near = swapped(middle_near, False)
    from_far = swapped(middle_far, True)
    product, sums = call(
        product_kernel,
        "product",
        (field, shape(16, 128, F32)),
        (mid, from_near, from_far, from_w, from_e, partial, w_send, d, r),
    )
    sums = sums_everywhere(sums)
    outs = call(final_kernel, "final", (field,) * 3, (sums, x, r, d, product))
    return tuple(out.reshape(x_field.shape) for out in outs)


def solution(mesh):
    field = P("lat", "lon", None, None)
    flat = P("lat", "lon", None)
    return jax.shard_map(
        body,
        mesh=mesh,
        in_specs=(field,) * 5 + (flat,) * 3 + (P(),) * 6,
        out_specs=(field,) * 3,
        check_vma=False,
    )
```

```python
import jax
import jax.numpy as jnp
from jax import lax
from jax.experimental import pallas as pl
from jax.experimental.pallas import tpu as pltpu
from jax.sharding import PartitionSpec as P

BF = jnp.bfloat16
F32 = jnp.float32
VMEM_LIMIT = 12 * 1024 * 1024


def dot(left, right):
    return jnp.dot(left, right, preferred_element_type=F32)


def dot_back(left, weight):
    return lax.dot_general(left, weight, (((1,), (1,)), ((), ())), preferred_element_type=F32)


def silu_slope(value):
    sig = 0.5 * jnp.tanh(0.5 * value) + 0.5
    return sig * (1.0 + value * (1.0 - sig))


def call(kernel, name, out_shape, args, scratch=(), hbm=None, cost=None):
    here = pl.BlockSpec(memory_space=pltpu.VMEM)
    there = pl.BlockSpec(memory_space=pltpu.HBM)
    first = len(args) if hbm is None else hbm
    away = [pltpu.with_memory_space_constraint(arg, pltpu.HBM) for arg in args[first:]]
    return pl.pallas_call(
        kernel,
        out_shape=out_shape,
        in_specs=[here] * first + [there] * len(away),
        out_specs=jax.tree.map(lambda _: here, out_shape),
        scratch_shapes=scratch,
        compiler_params=pltpu.CompilerParams(vmem_limit_bytes=VMEM_LIMIT),
        cost_estimate=cost,
        name=name,
    )(*args[:first], *away)


def shape(rows, cols, kind):
    return jax.ShapeDtypeStruct((rows, cols), kind)


def start_all(pairs, sems):
    copies = [pltpu.make_async_copy(a, b, sems.at[k]) for k, (a, b) in enumerate(pairs)]
    for copy in copies:
        copy.start()
    return copies


def slot_blocks():
    near = 1 - 2 * lax.rem(lax.axis_index("lat"), 2)
    inner = 1 - 2 * lax.rem(lax.axis_index("lon"), 2)
    places = (
        (-near, -inner), (-near, inner), (near, -inner), (near, inner), (near, 0), (-near, 0),
        (0, -inner), (0, inner), (0, 0),
    )
    return [(lat + 1) * 3 + lon + 1 for lat, lon in places]


def send_kernel(senders, receivers, obs_hbm, d_hbm, w_hbm, own, send_row, recv_row, obs, d, w, sems):
    pairs = ((d_hbm, d), (w_hbm, w), (senders, send_row), (receivers, recv_row), (obs_hbm, obs))
    for copy in start_all(pairs, sems):
        copy.wait()
    own[...] = dot(d[...].astype(BF), w[...]).astype(BF)


def prepare_kernel(
    send_row, recv_row, act_hbm, a_node_hbm, w_recv_hbm, w_self_hbm, w_edge_hbm, w_msg_hbm, w_out_hbm,
    pick, pick_t, act, a_node, w_recv, w_self, w_edge, w_msg, w_out, sems,
):
    pairs = (
        (act_hbm, act), (a_node_hbm, a_node), (w_recv_hbm, w_recv), (w_self_hbm, w_self),
        (w_edge_hbm, w_edge), (w_msg_hbm, w_msg), (w_out_hbm, w_out),
    )
    copies = start_all(pairs, sems)
    edges = act.shape[0]
    nodes = 128
    rows = lax.broadcasted_iota(jnp.int32, (nodes, edges), 0)
    lanes = lax.broadcasted_iota(jnp.int32, (edges, nodes), 1)
    sends = jnp.broadcast_to(send_row[...], (nodes, edges))
    recvs = jnp.broadcast_to(recv_row[...], (nodes, edges))
    s_row = sends - rows
    s_col = jnp.transpose(sends) - lanes
    r_col = jnp.transpose(recvs)
    blocks = slot_blocks()
    for k, b in enumerate(blocks):
        pick[:, k * nodes : (k + 1) * nodes] = jnp.where(s_col == b * nodes, 1.0, 0.0).astype(BF)
        pick_t[k * nodes : (k + 1) * nodes, :] = jnp.where(s_row == b * nodes, 1.0, 0.0).astype(BF)
    k = len(blocks)
    pick[:, k * nodes :] = jnp.where(r_col == lanes, 1.0, 0.0).astype(BF)
    pick_t[k * nodes :, :] = jnp.where(recvs == rows, 1.0, 0.0).astype(BF)
    for copy in copies:
        copy.wait()


def stack_kernel(outer, inner, after, beside):
    beside[0:128, :] = outer[...]
    beside[128:256, :] = inner[...]


def base_kernel(
    d, own, far, near, beside, pick, act, a_node, w_recv, w_self, w_edge, w_msg, w_out,
    base, slope, node_slope, self_pre, fold, gram, d_back, table,
):
    d_bf = d[...].astype(BF)
    table[0:128, :] = near[...]
    table[128:256, :] = far[...]
    table[256:384, :] = own[...]
    table[384:512, :] = dot(d_bf, w_recv[...]).astype(BF)
    base[...] = (
        dot(pick[:, 512:768], table[:256, :])
        + dot(pick[:, 768:1024], beside[...])
        + dot(pick[:, 1024:1280], table[256:, :])
    )
    slope[...] = silu_slope(act[...].astype(F32))
    node_slope[...] = silu_slope(a_node[...].astype(F32))
    self_pre[...] = dot(d_bf, w_self[...])
    fold[...] = dot(w_edge[...], w_msg[...]).astype(BF)
    gram[...] = dot_back(w_out[...], w_out[...]).astype(BF)
    d_back[...] = dot_back(d_bf, w_out[...])


def lanes_of(row, width):
    nodes = row.shape[1]
    column = jnp.transpose(jnp.broadcast_to(row, (nodes, nodes)))
    return jnp.concatenate([column] * (width // nodes), axis=1)


def main_kernel(
    from_far, from_near, base, slope, pick, pick_t, node_slope, self_pre, fold, gram, d_back, obs,
    corner_far, corner_near, edge_grad, node_grad, node_hidden,
):
    gathered = (
        base[...] + dot(pick[:, 0:256], from_far[...]) + dot(pick[:, 256:512], from_near[...])
    )
    hidden = (slope[...] * gathered).astype(BF)
    hidden_sum = dot(pick_t[1152:, :], hidden).astype(BF)
    pre_node = self_pre[...] + dot(hidden_sum, fold[...])
    inner = (node_slope[...] * pre_node).astype(BF)
    node_hidden[...] = inner
    back = lanes_of(obs[...], inner.shape[1]) * (d_back[...] + dot(inner, gram[...]))
    grad = (back * node_slope[...]).astype(BF)
    node_grad[...] = grad
    edge_back = dot_back(grad, fold[...]).astype(BF)
    e_grad = (dot(pick[:, 1152:], edge_back) * slope[...]).astype(BF)
    edge_grad[...] = e_grad
    corner_far[...] = dot(pick_t[0:256, :], e_grad).astype(BF)
    corner_near[...] = dot(pick_t[256:512, :], e_grad).astype(BF)


def rest_kernel(
    edge_grad, pick_t, node_grad, node_hidden, obs, d, w_recv, w_self, w_out,
    middle_far, middle_near, mid, partial,
):
    sums = dot(pick_t[512:, :], edge_grad[...])
    middle_near[...] = sums[:128, :].astype(BF)
    middle_far[...] = sums[128:256, :].astype(BF)
    mid[...] = sums[256:640, :]
    search = d[...]
    changed = search + dot(node_hidden[...], w_out[...])
    observed = lanes_of(obs[...], search.shape[1]) * changed
    back = dot_back(node_grad[...], w_self[...]) + dot_back(sums[640:, :].astype(BF), w_recv[...])
    partial[...] = search + observed + back


def merge_kernel(mid, from_far, from_near, to_outer, to_inner):
    for rows, out in ((slice(0, 128), to_outer), (slice(128, 256), to_inner)):
        out[...] = (
            mid[rows, :] + from_near[rows, :].astype(F32) + from_far[rows, :].astype(F32)
        ).astype(BF)


def product_kernel(
    mid, from_near, from_far, from_outer, from_inner, partial, w_send, d, r, product, sums
):
    total = mid[256:384, :]
    for part in (from_near, from_far, from_inner, from_outer):
        total = total + part[...].astype(F32)
    prod = partial[...] + dot_back(total.astype(BF), w_send[...])
    product[...] = prod
    res = r[...]
    lane = lax.broadcasted_iota(jnp.int32, sums.shape, 1)
    out = jnp.zeros(sums.shape, F32)
    for k, value in enumerate((res * res, d[...] * prod, res * prod, prod * prod)):
        out = jnp.where(lane == k, jnp.sum(value), out)
    sums[...] = out


def final_kernel(sums, x, r, d, product, new_x, new_r, new_d):
    total = jnp.sum(sums[...], axis=0, keepdims=True)
    norm_now, curvature = total[:, 0:1], total[:, 1:2]
    cross, square = total[:, 2:3], total[:, 3:4]
    alpha = norm_now / curvature
    norm_next = jnp.maximum(norm_now + alpha * (alpha * square - 2.0 * cross), 0.0)
    beta = norm_next / norm_now
    search = d[...]
    new_x[...] = x[...] + alpha * search
    left = r[...] - alpha * product[...]
    new_r[...] = left
    new_d[...] = left + beta * search


def swapped(value, axis, across):
    count = lax.axis_size(axis)
    first = 1 if across else 0
    last = count - 1 if axis == "lat" else count
    pairs = [(i, (i + 1) % count) for i in range(first, last, 2)]
    return lax.ppermute(value, axis, pairs + [(b, a) for a, b in pairs])


def sums_everywhere(value):
    n_lat, n_lon = lax.axis_size("lat"), lax.axis_size("lon")
    near = n_lon // 4
    first = [
        [(2 * y + c) * n_lon + x * near + z for c in range(2) for z in range(near)]
        for y in range(n_lat // 2)
        for x in range(4)
    ]
    second = [
        [(2 * y + c) * n_lon + x * near + z for y in range(n_lat // 2) for x in range(4)]
        for c in range(2)
        for z in range(near)
    ]
    value = lax.all_to_all(value, ("lat", "lon"), 0, 0, tiled=True, axis_index_groups=first)
    value = jnp.sum(value, axis=0, keepdims=True)
    value = jnp.broadcast_to(value, (len(second[0]), value.shape[1]))
    return lax.all_to_all(value, ("lat", "lon"), 0, 0, tiled=True, axis_index_groups=second)


def body(
    x_field, residual, direction, a_node, a_edge, senders, receivers, obs_weight,
    w_send, w_recv, w_edge_out, w_node_self, w_node_msg, w_node_out,
):
    nodes, width = x_field.shape[2:]
    edges = a_edge.shape[2]
    x = x_field.reshape(nodes, width)
    r = residual.reshape(nodes, width)
    d_hbm = direction.reshape(nodes, width)
    field = shape(nodes, width, F32)
    block = shape(nodes, width, BF)
    weight = shape(width, width, BF)
    own, send_row, recv_row, obs, d = call(
        send_kernel,
        "send_term",
        (
            block,
            shape(1, edges, jnp.int32),
            shape(1, edges, jnp.int32),
            shape(1, nodes, F32),
            field,
        ),
        (senders.reshape(1, edges), receivers.reshape(1, edges), obs_weight.reshape(1, nodes), d_hbm, w_send),
        hbm=0,
        scratch=(pltpu.VMEM((width, width), BF), pltpu.SemaphoreType.DMA((5,))),
    )
    outer = swapped(own, "lon", True)
    inner = swapped(own, "lon", False)
    far = swapped(own, "lat", True)
    near = swapped(own, "lat", False)
    pick, pick_t, act, node_act, w_recv, w_self, w_edge, w_msg, w_out = call(
        prepare_kernel,
        "prepare",
        (
            shape(edges, 10 * nodes, BF),
            shape(10 * nodes, edges, BF),
            shape(edges, width, BF),
            block,
        )
        + (weight,) * 5,
        (
            send_row, recv_row, a_edge.reshape(edges, width), a_node.reshape(nodes, width),
            w_recv, w_node_self, w_edge_out, w_node_msg, w_node_out,
        ),
        hbm=2,
        scratch=(pltpu.SemaphoreType.DMA((7,)),),
    )
    pair = shape(2 * nodes, width, BF)
    beside = call(stack_kernel, "stack", pair, (outer, inner, node_act))
    from_far = swapped(beside, "lat", True)
    from_near = swapped(beside, "lat", False)
    base, slope, node_slope, self_pre, fold, gram, d_back = call(
        base_kernel,
        "base",
        (shape(edges, width, F32),) * 2 + (field, field, weight, weight, field),
        (d, own, far, near, beside, pick, act, node_act, w_recv, w_self, w_edge, w_msg, w_out),
        scratch=(pltpu.VMEM((4 * nodes, width), BF),),
        cost=pl.CostEstimate(flops=5 * 10**9, bytes_accessed=5 * 10**7, transcendentals=0),
    )
    corner_far, corner_near, edge_grad, node_grad, node_hidden = call(
        main_kernel,
        "main",
        (pair, pair, shape(edges, width, BF), block, block),
        (
            from_far, from_near, base, slope, pick, pick_t, node_slope, self_pre, fold, gram, d_back, obs,
        ),
    )
    from_far = swapped(corner_far, "lat", True)
    from_near = swapped(corner_near, "lat", False)
    middle_far, middle_near, mid, partial = call(
        rest_kernel,
        "rest",
        (block, block, shape(3 * nodes, width, F32), field),
        (edge_grad, pick_t, node_grad, node_hidden, obs, d, w_recv, w_self, w_out),
        cost=pl.CostEstimate(flops=5 * 10**9, bytes_accessed=5 * 10**7, transcendentals=0),
    )
    to_outer, to_inner = call(merge_kernel, "merge", (block, block), (mid, from_far, from_near))
    from_outer = swapped(to_outer, "lon", True)
    from_inner = swapped(to_inner, "lon", False)
    from_far = swapped(middle_far, "lat", True)
    from_near = swapped(middle_near, "lat", False)
    product, sums = call(
        product_kernel,
        "product",
        (field, shape(16, 128, F32)),
        (mid, from_near, from_far, from_outer, from_inner, partial, w_send, d, r),
    )
    sums = sums_everywhere(sums)
    outs = call(final_kernel, "final", (field,) * 3, (sums, x, r, d, product))
    return tuple(out.reshape(x_field.shape) for out in outs)


def solution(mesh):
    field = P("lat", "lon", None, None)
    flat = P("lat", "lon", None)
    return jax.shard_map(
        body,
        mesh=mesh,
        in_specs=(field,) * 5 + (flat,) * 3 + (P(),) * 6,
        out_specs=(field,) * 3,
        check_vma=False,
    )
```

```python
import functools

import jax
import jax.numpy as jnp
from jax import lax
from jax.experimental import pallas as pl
from jax.experimental.pallas import tpu as pltpu
from jax.sharding import PartitionSpec as P

BF = jnp.bfloat16
F32 = jnp.float32
LIGHT = 10**9
HEAVY = 5 * 10**9
VMEM_LIMIT = 12 * 1024 * 1024


def dot(left, right):
    return jnp.dot(left, right, preferred_element_type=F32)


def dot_back(left, weight):
    return lax.dot_general(left, weight, (((1,), (1,)), ((), ())), preferred_element_type=F32)


def silu_slope(value):
    sig = 0.5 * jnp.tanh(0.5 * value) + 0.5
    return sig * (1.0 + value * (1.0 - sig))


def call(kernel, name, out_shape, args, scratch=(), hbm=None, cost=None):
    here = pl.BlockSpec(memory_space=pltpu.VMEM)
    there = pl.BlockSpec(memory_space=pltpu.HBM)
    first = len(args) if hbm is None else hbm
    away = [pltpu.with_memory_space_constraint(arg, pltpu.HBM) for arg in args[first:]]
    return pl.pallas_call(
        kernel,
        out_shape=out_shape,
        in_specs=[here] * first + [there] * len(away),
        out_specs=jax.tree.map(lambda _: here, out_shape),
        scratch_shapes=scratch,
        compiler_params=pltpu.CompilerParams(vmem_limit_bytes=VMEM_LIMIT),
        cost_estimate=cost,
        name=name,
    )(*args[:first], *away)


def cost(flops):
    return pl.CostEstimate(flops=flops, bytes_accessed=flops // 100, transcendentals=0)


def shape(rows, cols, kind):
    return jax.ShapeDtypeStruct((rows, cols), kind)


def start_all(pairs, sems):
    copies = [pltpu.make_async_copy(a, b, sems.at[k]) for k, (a, b) in enumerate(pairs)]
    for copy in copies:
        copy.start()
    return copies


def slot_blocks():
    near = 1 - 2 * lax.rem(lax.axis_index("lat"), 2)
    inner = 1 - 2 * lax.rem(lax.axis_index("lon"), 2)
    places = (
        (-near, -inner), (-near, inner), (near, -inner), (near, inner), (near, 0), (-near, 0),
        (0, -inner), (0, inner), (0, 0),
    )
    return [(lat + 1) * 3 + lon + 1 for lat, lon in places]


def send_kernel(senders, receivers, obs_hbm, d_hbm, w_hbm, own, send_row, recv_row, obs, d, w, sems):
    pairs = ((d_hbm, d), (w_hbm, w), (senders, send_row), (receivers, recv_row), (obs_hbm, obs))
    for copy in start_all(pairs, sems):
        copy.wait()
    own[...] = dot(d[...].astype(BF), w[...]).astype(BF)


def prepare_kernel(
    send_row, recv_row, d, act_hbm, a_node_hbm, w_recv_hbm, w_self_hbm, w_edge_hbm, w_msg_hbm, w_out_hbm,
    pick, pick_t, act, a_node, recv_term, w_recv, w_self, w_edge, w_msg, w_out, sems,
):
    pairs = (
        (w_recv_hbm, w_recv), (w_self_hbm, w_self), (w_out_hbm, w_out), (w_edge_hbm, w_edge),
        (w_msg_hbm, w_msg), (a_node_hbm, a_node), (act_hbm, act),
    )
    copies = start_all(pairs, sems)
    edges = act.shape[0]
    nodes = 128
    rows = lax.broadcasted_iota(jnp.int32, (nodes, edges), 0)
    lanes = lax.broadcasted_iota(jnp.int32, (edges, nodes), 1)
    sends = jnp.broadcast_to(send_row[...], (nodes, edges))
    recvs = jnp.broadcast_to(recv_row[...], (nodes, edges))
    s_row = sends - rows
    s_col = jnp.transpose(sends) - lanes
    r_col = jnp.transpose(recvs)
    blocks = slot_blocks()
    for k, b in enumerate(blocks):
        pick[:, k * nodes : (k + 1) * nodes] = jnp.where(s_col == b * nodes, 1.0, 0.0).astype(BF)
        pick_t[k * nodes : (k + 1) * nodes, :] = jnp.where(s_row == b * nodes, 1.0, 0.0).astype(BF)
    k = len(blocks)
    pick[:, k * nodes :] = jnp.where(r_col == lanes, 1.0, 0.0).astype(BF)
    pick_t[k * nodes :, :] = jnp.where(recvs == rows, 1.0, 0.0).astype(BF)
    for copy in copies:
        copy.wait()
    d_bf = d[...].astype(BF)
    recv_term[...] = dot(d_bf, w_recv[...]).astype(BF)


def pass_kernel(block, after, out):
    out[...] = block[...]


def stack_kernel(outer, inner, outer_out, pair):
    outer_out[...] = outer[...]
    pair[0:128, :] = outer[...]
    pair[128:256, :] = inner[...]


def gathered(pick, first, parts, table):
    row = 0
    for part in parts:
        table[row : row + part.shape[0], :] = part[...]
        row += part.shape[0]
    return dot(pick[:, first : first + row], table[...])


def base_kernel(
    far, near, outer, inner, own, recv_term, pick, act, a_node, d, w_self, w_edge, w_msg, w_out,
    base, slope, node_slope, self_pre, d_back, fold, gram, table,
):
    d_bf = d[...].astype(BF)
    self_pre[...] = dot(d_bf, w_self[...])
    d_back[...] = dot_back(d_bf, w_out[...])
    fold[...] = dot(w_edge[...], w_msg[...]).astype(BF)
    gram[...] = dot_back(w_out[...], w_out[...]).astype(BF)
    slope[...] = silu_slope(act[...].astype(F32))
    node_slope[...] = silu_slope(a_node[...].astype(F32))
    base[...] = gathered(pick, 512, (near, far, outer, inner, own, recv_term), table)


def more_kernel(first, part, base, pick, more):
    more[...] = base[...] + dot(pick[:, first : first + part.shape[0]], part[...])


def lanes_of(row, width):
    nodes = row.shape[1]
    column = jnp.transpose(jnp.broadcast_to(row, (nodes, nodes)))
    return jnp.concatenate([column] * (width // nodes), axis=1)


def main_kernel(
    far_outer, base, slope, pick, pick_t, node_slope, self_pre, fold, gram, d_back, obs,
    corner_outer, corner_inner, all_near, edge_grad, node_grad, node_hidden,
):
    edge_input = base[...] + dot(pick[:, 0:128], far_outer[...])
    hidden = (slope[...] * edge_input).astype(BF)
    hidden_sum = dot(pick_t[1152:, :], hidden).astype(BF)
    pre_node = self_pre[...] + dot(hidden_sum, fold[...])
    inner = (node_slope[...] * pre_node).astype(BF)
    node_hidden[...] = inner
    back = lanes_of(obs[...], inner.shape[1]) * (d_back[...] + dot(inner, gram[...]))
    grad = (back * node_slope[...]).astype(BF)
    node_grad[...] = grad
    edge_back = dot_back(grad, fold[...]).astype(BF)
    e_grad = (dot(pick[:, 1152:], edge_back) * slope[...]).astype(BF)
    edge_grad[...] = e_grad
    sums = dot(pick_t[0:640, :], e_grad).astype(BF)
    corner_outer[...] = sums[0:128, :]
    corner_inner[...] = sums[128:256, :]
    all_near[...] = sums[256:640, :]


def rest_kernel(
    edge_grad, pick_t, node_grad, node_hidden, obs, d, w_recv, w_self, w_out,
    middle_far, mid, partial,
):
    sums = dot(pick_t[640:, :], edge_grad[...])
    middle_far[...] = sums[:128, :].astype(BF)
    mid[...] = sums[128:512, :]
    search = d[...]
    changed = search + dot(node_hidden[...], w_out[...])
    observed = lanes_of(obs[...], search.shape[1]) * changed
    back = dot_back(node_grad[...], w_self[...]) + dot_back(sums[512:, :].astype(BF), w_recv[...])
    partial[...] = search + observed + back


def merge_kernel(first, mid, from_far, from_near, *refs):
    rows = slice(first, first + 128)
    total = mid[rows, :] + from_far[...].astype(F32) + from_near[rows, :].astype(F32)
    refs[-1][...] = total.astype(BF)


def center_kernel(mid, from_outer, center):
    center[...] = mid[256:384, :] + from_outer[...].astype(F32)


def product_kernel(
    center, from_near, from_far, from_inner, partial, w_send, d, r, product, sums
):
    total = center[...] + from_near[256:384, :].astype(F32)
    for part in (from_far, from_inner):
        total = total + part[...].astype(F32)
    prod = partial[...] + dot_back(total.astype(BF), w_send[...])
    product[...] = prod
    res = r[...]
    lane = lax.broadcasted_iota(jnp.int32, sums.shape, 1)
    out = jnp.zeros(sums.shape, F32)
    for k, value in enumerate((res * res, d[...] * prod, res * prod, prod * prod)):
        out = jnp.where(lane == k, jnp.sum(value), out)
    sums[...] = out


def final_kernel(sums, x, r, d, product, new_x, new_r, new_d):
    total = jnp.sum(sums[...], axis=0, keepdims=True)
    norm_now, curvature = total[:, 0:1], total[:, 1:2]
    cross, square = total[:, 2:3], total[:, 3:4]
    alpha = norm_now / curvature
    norm_next = jnp.maximum(norm_now + alpha * (alpha * square - 2.0 * cross), 0.0)
    beta = norm_next / norm_now
    search = d[...]
    new_x[...] = x[...] + alpha * search
    left = r[...] - alpha * product[...]
    new_r[...] = left
    new_d[...] = left + beta * search


def swapped(value, axis, across):
    n_lat, n_lon = lax.axis_size("lat"), lax.axis_size("lon")

    def partner(i, j):
        if axis == "lon":
            return i, (j - 1 if j % 2 == 0 else j + 1) % n_lon if across else j ^ 1
        if not across:
            return i ^ 1, j
        return (i, j ^ 1) if i in (0, n_lat - 1) else (i - 1 if i % 2 == 0 else i + 1, j)

    pairs = []
    for i in range(n_lat):
        for j in range(n_lon):
            to_lat, to_lon = partner(i, j)
            pairs.append((i * n_lon + j, to_lat * n_lon + to_lon))
    return lax.ppermute(value, ("lat", "lon"), pairs)


def sums_everywhere(value):
    n_lat, n_lon = lax.axis_size("lat"), lax.axis_size("lon")
    near = n_lon // 4
    first = [
        [(2 * y + c) * n_lon + x * near + z for c in range(2) for z in range(near)]
        for y in range(n_lat // 2)
        for x in range(4)
    ]
    second = [
        [(2 * y + c) * n_lon + x * near + z for y in range(n_lat // 2) for x in range(4)]
        for c in range(2)
        for z in range(near)
    ]
    value = lax.all_to_all(value, ("lat", "lon"), 0, 0, tiled=True, axis_index_groups=first)
    value = jnp.sum(value, axis=0, keepdims=True)
    value = jnp.broadcast_to(value, (len(second[0]), value.shape[1]))
    return lax.all_to_all(value, ("lat", "lon"), 0, 0, tiled=True, axis_index_groups=second)


def body(
    x_field, residual, direction, a_node, a_edge, senders, receivers, obs_weight,
    w_send, w_recv, w_edge_out, w_node_self, w_node_msg, w_node_out,
):
    nodes, width = x_field.shape[2:]
    edges = a_edge.shape[2]
    x = x_field.reshape(nodes, width)
    r = residual.reshape(nodes, width)
    d_hbm = direction.reshape(nodes, width)
    field = shape(nodes, width, F32)
    block = shape(nodes, width, BF)
    weight = shape(width, width, BF)
    own, send_row, recv_row, obs, d = call(
        send_kernel,
        "send_term",
        (
            block,
            shape(1, edges, jnp.int32),
            shape(1, edges, jnp.int32),
            shape(1, nodes, F32),
            field,
        ),
        (senders.reshape(1, edges), receivers.reshape(1, edges), obs_weight.reshape(1, nodes), d_hbm, w_send),
        hbm=0,
        scratch=(pltpu.VMEM((width, width), BF), pltpu.SemaphoreType.DMA((5,))),
    )
    outer = swapped(own, "lon", True)
    inner = swapped(own, "lon", False)
    far = swapped(own, "lat", True)
    near = swapped(own, "lat", False)
    pick, pick_t, act, node_act, recv_term, w_recv, w_self, w_edge, w_msg, w_out = call(
        prepare_kernel,
        "prepare",
        (
            shape(edges, 10 * nodes, BF),
            shape(10 * nodes, edges, BF),
            shape(edges, width, BF),
            block,
            block,
        )
        + (weight,) * 5,
        (
            send_row, recv_row, d, a_edge.reshape(edges, width), a_node.reshape(nodes, width),
            w_recv, w_node_self, w_edge_out, w_node_msg, w_node_out,
        ),
        hbm=3,
        scratch=(
            pltpu.SemaphoreType.DMA((7,)),
        ),
    )
    pair = shape(2 * nodes, width, BF)
    inner = call(pass_kernel, "pass_inner", block, (inner, recv_term))
    far_inner = swapped(inner, "lat", True)
    outer, beside = call(stack_kernel, "stack", (block, pair), (outer, inner))
    far_outer = swapped(outer, "lat", True)
    near_pair = swapped(beside, "lat", False)
    base, slope, node_slope, self_pre, d_back, fold, gram = call(
        base_kernel,
        "base",
        (shape(edges, width, F32),) * 2 + (field, field, field, weight, weight),
        (far, near, outer, inner, own, recv_term, pick, act, node_act, d, w_self, w_edge, w_msg, w_out),
        scratch=(pltpu.VMEM((6 * nodes, width), BF),),
        cost=cost(LIGHT),
    )
    base = call(
        functools.partial(more_kernel, 128),
        "inner",
        shape(edges, width, F32),
        (far_inner, base, pick),
        cost=cost(HEAVY),
    )
    base = call(
        functools.partial(more_kernel, 256), "near", shape(edges, width, F32), (near_pair, base, pick)
    )
    corner_outer, corner_inner, all_near, edge_grad, node_grad, node_hidden = call(
        main_kernel,
        "main",
        (block, block, shape(3 * nodes, width, BF), shape(edges, width, BF), block, block),
        (far_outer, base, slope, pick, pick_t, node_slope, self_pre, fold, gram, d_back, obs),
    )
    far_outer = swapped(corner_outer, "lat", True)
    far_inner = swapped(corner_inner, "lat", True)
    from_near = swapped(all_near, "lat", False)
    middle_far, mid, partial = call(
        rest_kernel,
        "rest",
        (block, shape(3 * nodes, width, F32), field),
        (edge_grad, pick_t, node_grad, node_hidden, obs, d, w_recv, w_self, w_out),
        cost=cost(HEAVY),
    )
    to_outer = call(
        functools.partial(merge_kernel, 0), "merge_outer", block, (mid, far_outer, from_near)
    )
    to_inner = call(
        functools.partial(merge_kernel, 128), "merge_inner", block, (mid, far_inner, from_near, to_outer)
    )
    from_outer = swapped(to_outer, "lon", True)
    from_inner = swapped(to_inner, "lon", False)
    from_far = swapped(middle_far, "lat", True)
    center = call(
        center_kernel,
        "center",
        field,
        (mid, from_outer),
        cost=cost(HEAVY),
    )
    product, sums = call(
        product_kernel,
        "product",
        (field, shape(16, 128, F32)),
        (center, from_near, from_far, from_inner, partial, w_send, d, r),
    )
    sums = sums_everywhere(sums)
    outs = call(final_kernel, "final", (field,) * 3, (sums, x, r, d, product))
    return tuple(out.reshape(x_field.shape) for out in outs)


def solution(mesh):
    field = P("lat", "lon", None, None)
    flat = P("lat", "lon", None)
    return jax.shard_map(
        body,
        mesh=mesh,
        in_specs=(field,) * 5 + (flat,) * 3 + (P(),) * 6,
        out_specs=(field,) * 3,
        check_vma=False,
    )
```

```python
import functools

import jax
import jax.numpy as jnp
from jax import lax
from jax.experimental import pallas as pl
from jax.experimental.pallas import tpu as pltpu
from jax.sharding import PartitionSpec as P

BF = jnp.bfloat16
F32 = jnp.float32
LIGHT = 10**9
HEAVY = 5 * 10**9
VMEM_LIMIT = 12 * 1024 * 1024


def dot(left, right):
    return jnp.dot(left, right, preferred_element_type=F32)


def dot_back(left, weight):
    return lax.dot_general(left, weight, (((1,), (1,)), ((), ())), preferred_element_type=F32)


def silu_slope(value):
    sig = 0.5 * jnp.tanh(0.5 * value) + 0.5
    return sig * (1.0 + value * (1.0 - sig))


def call(kernel, name, out_shape, args, scratch=(), hbm=None, cost=None):
    here = pl.BlockSpec(memory_space=pltpu.VMEM)
    there = pl.BlockSpec(memory_space=pltpu.HBM)
    first = len(args) if hbm is None else hbm
    away = [pltpu.with_memory_space_constraint(arg, pltpu.HBM) for arg in args[first:]]
    return pl.pallas_call(
        kernel,
        out_shape=out_shape,
        in_specs=[here] * first + [there] * len(away),
        out_specs=jax.tree.map(lambda _: here, out_shape),
        scratch_shapes=scratch,
        compiler_params=pltpu.CompilerParams(vmem_limit_bytes=VMEM_LIMIT),
        cost_estimate=cost,
        name=name,
    )(*args[:first], *away)


def cost(flops):
    return pl.CostEstimate(flops=flops, bytes_accessed=flops // 100, transcendentals=0)


def shape(rows, cols, kind):
    return jax.ShapeDtypeStruct((rows, cols), kind)


def start_all(pairs, sems):
    copies = [pltpu.make_async_copy(a, b, sems.at[k]) for k, (a, b) in enumerate(pairs)]
    for copy in copies:
        copy.start()
    return copies


def slot_blocks():
    near = 1 - 2 * lax.rem(lax.axis_index("lat"), 2)
    inner = 1 - 2 * lax.rem(lax.axis_index("lon"), 2)
    places = (
        (-near, -inner), (near, -inner), (-near, inner), (near, inner), (near, 0), (-near, 0),
        (0, -inner), (0, inner), (0, 0),
    )
    return [(lat + 1) * 3 + lon + 1 for lat, lon in places]


def send_kernel(senders, receivers, obs_hbm, d_hbm, w_hbm, own, send_row, recv_row, obs, d, w, sems):
    pairs = ((d_hbm, d), (w_hbm, w), (senders, send_row), (receivers, recv_row), (obs_hbm, obs))
    for copy in start_all(pairs, sems):
        copy.wait()
    own[...] = dot(d[...].astype(BF), w[...]).astype(BF)


def prepare_kernel(
    send_row, recv_row, d, act_hbm, a_node_hbm, w_recv_hbm, w_self_hbm, w_edge_hbm, w_msg_hbm, w_out_hbm,
    pick, pick_t, act, a_node, recv_term, w_recv, w_self, w_edge, w_msg, w_out, sems,
):
    pairs = (
        (w_recv_hbm, w_recv), (w_self_hbm, w_self), (w_out_hbm, w_out), (w_edge_hbm, w_edge),
        (w_msg_hbm, w_msg), (a_node_hbm, a_node), (act_hbm, act),
    )
    copies = start_all(pairs, sems)
    edges = act.shape[0]
    nodes = 128
    rows = lax.broadcasted_iota(jnp.int32, (nodes, edges), 0)
    lanes = lax.broadcasted_iota(jnp.int32, (edges, nodes), 1)
    sends = jnp.broadcast_to(send_row[...], (nodes, edges))
    recvs = jnp.broadcast_to(recv_row[...], (nodes, edges))
    s_row = sends - rows
    s_col = jnp.transpose(sends) - lanes
    r_col = jnp.transpose(recvs)
    blocks = slot_blocks()
    for k, b in enumerate(blocks):
        pick[:, k * nodes : (k + 1) * nodes] = jnp.where(s_col == b * nodes, 1.0, 0.0).astype(BF)
        pick_t[k * nodes : (k + 1) * nodes, :] = jnp.where(s_row == b * nodes, 1.0, 0.0).astype(BF)
    k = len(blocks)
    pick[:, k * nodes :] = jnp.where(r_col == lanes, 1.0, 0.0).astype(BF)
    pick_t[k * nodes :, :] = jnp.where(recvs == rows, 1.0, 0.0).astype(BF)
    for copy in copies:
        copy.wait()
    d_bf = d[...].astype(BF)
    recv_term[...] = dot(d_bf, w_recv[...]).astype(BF)


def pass_kernel(block, after, out):
    out[...] = block[...]


def gathered(pick, first, parts, table):
    row = 0
    for part in parts:
        table[row : row + part.shape[0], :] = part[...]
        row += part.shape[0]
    return dot(pick[:, first : first + row], table[...])


def base_kernel(
    far, near, outer, inner, own, recv_term, pick, act, a_node, d, w_self, w_edge, w_msg, w_out,
    base, slope, node_slope, self_pre, d_back, fold, gram, table,
):
    d_bf = d[...].astype(BF)
    self_pre[...] = dot(d_bf, w_self[...])
    d_back[...] = dot_back(d_bf, w_out[...])
    fold[...] = dot(w_edge[...], w_msg[...]).astype(BF)
    gram[...] = dot_back(w_out[...], w_out[...]).astype(BF)
    slope[...] = silu_slope(act[...].astype(F32))
    node_slope[...] = silu_slope(a_node[...].astype(F32))
    base[...] = gathered(pick, 512, (near, far, outer, inner, own, recv_term), table)


def inner_kernel(far_inner, near_inner, base, pick, more, table):
    more[...] = base[...] + gathered(pick, 256, (far_inner, near_inner), table)


def lanes_of(row, width):
    nodes = row.shape[1]
    column = jnp.transpose(jnp.broadcast_to(row, (nodes, nodes)))
    return jnp.concatenate([column] * (width // nodes), axis=1)


def main_kernel(
    far_outer, near_outer, base, slope, pick, pick_t, node_slope, self_pre, fold, gram, d_back, obs,
    corner_outer, edge_grad, node_grad, node_hidden, table,
):
    edge_input = base[...] + gathered(pick, 0, (far_outer, near_outer), table)
    hidden = (slope[...] * edge_input).astype(BF)
    hidden_sum = dot(pick_t[1152:, :], hidden).astype(BF)
    pre_node = self_pre[...] + dot(hidden_sum, fold[...])
    inner = (node_slope[...] * pre_node).astype(BF)
    node_hidden[...] = inner
    back = lanes_of(obs[...], inner.shape[1]) * (d_back[...] + dot(inner, gram[...]))
    grad = (back * node_slope[...]).astype(BF)
    node_grad[...] = grad
    edge_back = dot_back(grad, fold[...]).astype(BF)
    e_grad = (dot(pick[:, 1152:], edge_back) * slope[...]).astype(BF)
    edge_grad[...] = e_grad
    corner_outer[...] = dot(pick_t[0:128, :], e_grad).astype(BF)


def corner_kernel(edge_grad, pick_t, corner_inner, all_near):
    sums = dot(pick_t[128:640, :], edge_grad[...]).astype(BF)
    corner_inner[...] = sums[128:256, :]
    all_near[0:128, :] = sums[0:128, :]
    all_near[128:384, :] = sums[256:512, :]


def rest_kernel(
    edge_grad, pick_t, node_grad, node_hidden, obs, d, w_recv, w_self, w_out,
    middle_far, mid, partial,
):
    sums = dot(pick_t[640:, :], edge_grad[...])
    middle_far[...] = sums[:128, :].astype(BF)
    mid[...] = sums[128:512, :]
    search = d[...]
    changed = search + dot(node_hidden[...], w_out[...])
    observed = lanes_of(obs[...], search.shape[1]) * changed
    back = dot_back(node_grad[...], w_self[...]) + dot_back(sums[512:, :].astype(BF), w_recv[...])
    partial[...] = search + observed + back


def merge_kernel(first, mid, from_far, from_near, *refs):
    rows = slice(first, first + 128)
    total = mid[rows, :] + from_far[...].astype(F32) + from_near[rows, :].astype(F32)
    refs[-1][...] = total.astype(BF)


def center_kernel(mid, from_outer, center):
    center[...] = mid[256:384, :] + from_outer[...].astype(F32)


def product_kernel(
    center, from_near, from_inner, from_far, partial, w_send, d, r, product, sums
):
    total = center[...] + from_near[256:384, :].astype(F32)
    for part in (from_far, from_inner):
        total = total + part[...].astype(F32)
    prod = partial[...] + dot_back(total.astype(BF), w_send[...])
    product[...] = prod
    res = r[...]
    lane = lax.broadcasted_iota(jnp.int32, sums.shape, 1)
    out = jnp.zeros(sums.shape, F32)
    for k, value in enumerate((res * res, d[...] * prod, res * prod, prod * prod)):
        out = jnp.where(lane == k, jnp.sum(value), out)
    sums[...] = out


def final_kernel(sums, x, r, d, product, new_x, new_r, new_d):
    total = jnp.sum(sums[...], axis=0, keepdims=True)
    norm_now, curvature = total[:, 0:1], total[:, 1:2]
    cross, square = total[:, 2:3], total[:, 3:4]
    alpha = norm_now / curvature
    norm_next = jnp.maximum(norm_now + alpha * (alpha * square - 2.0 * cross), 0.0)
    beta = norm_next / norm_now
    search = d[...]
    new_x[...] = x[...] + alpha * search
    left = r[...] - alpha * product[...]
    new_r[...] = left
    new_d[...] = left + beta * search


def swapped(value, axis, across):
    n_lat, n_lon = lax.axis_size("lat"), lax.axis_size("lon")

    def partner(i, j):
        if axis == "lon":
            return i, (j - 1 if j % 2 == 0 else j + 1) % n_lon if across else j ^ 1
        if not across:
            return i ^ 1, j
        return (i, j ^ 1) if i in (0, n_lat - 1) else (i - 1 if i % 2 == 0 else i + 1, j)

    pairs = []
    for i in range(n_lat):
        for j in range(n_lon):
            to_lat, to_lon = partner(i, j)
            pairs.append((i * n_lon + j, to_lat * n_lon + to_lon))
    return lax.ppermute(value, ("lat", "lon"), pairs)


def sums_everywhere(value):
    n_lat, n_lon = lax.axis_size("lat"), lax.axis_size("lon")
    near = n_lon // 4
    first = [
        [(2 * y + c) * n_lon + x * near + z for c in range(2) for z in range(near)]
        for y in range(n_lat // 2)
        for x in range(4)
    ]
    second = [
        [(2 * y + c) * n_lon + x * near + z for y in range(n_lat // 2) for x in range(4)]
        for c in range(2)
        for z in range(near)
    ]
    value = lax.all_to_all(value, ("lat", "lon"), 0, 0, tiled=True, axis_index_groups=first)
    value = jnp.sum(value, axis=0, keepdims=True)
    value = jnp.broadcast_to(value, (len(second[0]), value.shape[1]))
    return lax.all_to_all(value, ("lat", "lon"), 0, 0, tiled=True, axis_index_groups=second)


def body(
    x_field, residual, direction, a_node, a_edge, senders, receivers, obs_weight,
    w_send, w_recv, w_edge_out, w_node_self, w_node_msg, w_node_out,
):
    nodes, width = x_field.shape[2:]
    edges = a_edge.shape[2]
    x = x_field.reshape(nodes, width)
    r = residual.reshape(nodes, width)
    d_hbm = direction.reshape(nodes, width)
    field = shape(nodes, width, F32)
    block = shape(nodes, width, BF)
    weight = shape(width, width, BF)
    own, send_row, recv_row, obs, d = call(
        send_kernel,
        "send_term",
        (
            block,
            shape(1, edges, jnp.int32),
            shape(1, edges, jnp.int32),
            shape(1, nodes, F32),
            field,
        ),
        (senders.reshape(1, edges), receivers.reshape(1, edges), obs_weight.reshape(1, nodes), d_hbm, w_send),
        hbm=0,
        scratch=(pltpu.VMEM((width, width), BF), pltpu.SemaphoreType.DMA((5,))),
    )
    outer = swapped(own, "lon", True)
    inner = swapped(own, "lon", False)
    far = swapped(own, "lat", True)
    near = swapped(own, "lat", False)
    pick, pick_t, act, node_act, recv_term, w_recv, w_self, w_edge, w_msg, w_out = call(
        prepare_kernel,
        "prepare",
        (
            shape(edges, 10 * nodes, BF),
            shape(10 * nodes, edges, BF),
            shape(edges, width, BF),
            block,
            block,
        )
        + (weight,) * 5,
        (
            send_row, recv_row, d, a_edge.reshape(edges, width), a_node.reshape(nodes, width),
            w_recv, w_node_self, w_edge_out, w_node_msg, w_node_out,
        ),
        hbm=3,
        scratch=(
            pltpu.SemaphoreType.DMA((7,)),
        ),
    )
    pair = shape(2 * nodes, width, BF)
    inner = call(pass_kernel, "pass_inner", block, (inner, recv_term))
    far_inner = swapped(inner, "lat", True)
    near_inner = swapped(inner, "lat", False)
    outer = call(pass_kernel, "pass_outer", block, (outer, inner))
    far_outer = swapped(outer, "lat", True)
    near_outer = swapped(outer, "lat", False)
    base, slope, node_slope, self_pre, d_back, fold, gram = call(
        base_kernel,
        "base",
        (shape(edges, width, F32),) * 2 + (field, field, field, weight, weight),
        (far, near, outer, inner, own, recv_term, pick, act, node_act, d, w_self, w_edge, w_msg, w_out),
        scratch=(pltpu.VMEM((6 * nodes, width), BF),),
        cost=cost(LIGHT),
    )
    base = call(
        inner_kernel,
        "inner",
        shape(edges, width, F32),
        (far_inner, near_inner, base, pick),
        scratch=(pltpu.VMEM((2 * nodes, width), BF),),
        cost=cost(HEAVY),
    )
    far_outer = call(pass_kernel, "gate", block, (far_outer, base), cost=cost(HEAVY))
    corner_outer, edge_grad, node_grad, node_hidden = call(
        main_kernel,
        "main",
        (block, shape(edges, width, BF), block, block),
        (
            far_outer, near_outer, base, slope, pick, pick_t, node_slope, self_pre, fold, gram, d_back, obs,
        ),
        scratch=(pltpu.VMEM((2 * nodes, width), BF),),
    )
    far_outer = swapped(corner_outer, "lat", True)
    corner_inner, all_near = call(
        corner_kernel, "corner", (block, shape(3 * nodes, width, BF)), (edge_grad, pick_t)
    )
    far_inner = swapped(corner_inner, "lat", True)
    from_near = swapped(all_near, "lat", False)
    middle_far, mid, partial = call(
        rest_kernel,
        "rest",
        (block, shape(3 * nodes, width, F32), field),
        (edge_grad, pick_t, node_grad, node_hidden, obs, d, w_recv, w_self, w_out),
        cost=cost(LIGHT // 100),
    )
    far_outer = call(pass_kernel, "gate", block, (far_outer, obs), cost=cost(HEAVY))
    to_outer = call(
        functools.partial(merge_kernel, 0), "merge_outer", block, (mid, far_outer, from_near)
    )
    to_inner = call(
        functools.partial(merge_kernel, 128), "merge_inner", block, (mid, far_inner, from_near, to_outer)
    )
    from_outer = swapped(to_outer, "lon", True)
    from_inner = swapped(to_inner, "lon", False)
    from_far = swapped(middle_far, "lat", True)
    center = call(
        center_kernel,
        "center",
        field,
        (mid, from_outer),
        cost=cost(HEAVY),
    )
    product, sums = call(
        product_kernel,
        "product",
        (field, shape(16, 128, F32)),
        (center, from_near, from_inner, from_far, partial, w_send, d, r),
    )
    sums = sums_everywhere(sums)
    outs = call(final_kernel, "final", (field,) * 3, (sums, x, r, d, product))
    return tuple(out.reshape(x_field.shape) for out in outs)


def solution(mesh):
    field = P("lat", "lon", None, None)
    flat = P("lat", "lon", None)
    return jax.shard_map(
        body,
        mesh=mesh,
        in_specs=(field,) * 5 + (flat,) * 3 + (P(),) * 6,
        out_specs=(field,) * 3,
        check_vma=False,
    )
```

```python
import functools

import jax
import jax.numpy as jnp
from jax import lax
from jax.experimental import pallas as pl
from jax.experimental.pallas import tpu as pltpu
from jax.sharding import PartitionSpec as P

BF = jnp.bfloat16
F32 = jnp.float32
LIGHT = 10**9
HEAVY = 5 * 10**9
VMEM_LIMIT = 12 * 1024 * 1024


def dot(left, right):
    return jnp.dot(left, right, preferred_element_type=F32)


def dot_back(left, weight):
    return lax.dot_general(left, weight, (((1,), (1,)), ((), ())), preferred_element_type=F32)


def silu_slope(value):
    sig = 0.5 * jnp.tanh(0.5 * value) + 0.5
    return sig * (1.0 + value * (1.0 - sig))


def call(kernel, name, out_shape, args, scratch=(), hbm=None, cost=None):
    here = pl.BlockSpec(memory_space=pltpu.VMEM)
    there = pl.BlockSpec(memory_space=pltpu.HBM)
    first = len(args) if hbm is None else hbm
    away = [pltpu.with_memory_space_constraint(arg, pltpu.HBM) for arg in args[first:]]
    return pl.pallas_call(
        kernel,
        out_shape=out_shape,
        in_specs=[here] * first + [there] * len(away),
        out_specs=jax.tree.map(lambda _: here, out_shape),
        scratch_shapes=scratch,
        compiler_params=pltpu.CompilerParams(vmem_limit_bytes=VMEM_LIMIT),
        cost_estimate=cost,
        name=name,
    )(*args[:first], *away)


def cost(flops):
    return pl.CostEstimate(flops=flops, bytes_accessed=flops // 100, transcendentals=0)


def shape(rows, cols, kind):
    return jax.ShapeDtypeStruct((rows, cols), kind)


def start_all(pairs, sems):
    copies = [pltpu.make_async_copy(a, b, sems.at[k]) for k, (a, b) in enumerate(pairs)]
    for copy in copies:
        copy.start()
    return copies


def slot_blocks():
    near = 1 - 2 * lax.rem(lax.axis_index("lat"), 2)
    inner = 1 - 2 * lax.rem(lax.axis_index("lon"), 2)
    places = (
        (-near, -inner), (near, -inner), (-near, inner), (near, inner), (near, 0), (-near, 0),
        (0, -inner), (0, inner), (0, 0),
    )
    return [(lat + 1) * 3 + lon + 1 for lat, lon in places]


def send_kernel(senders, receivers, obs_hbm, d_hbm, w_hbm, own, send_row, recv_row, obs, d, w, sems):
    pairs = ((d_hbm, d), (w_hbm, w), (senders, send_row), (receivers, recv_row), (obs_hbm, obs))
    for copy in start_all(pairs, sems):
        copy.wait()
    own[...] = dot(d[...].astype(BF), w[...]).astype(BF)


def prepare_kernel(
    send_row, recv_row, d, act_hbm, a_node_hbm, w_recv_hbm, w_self_hbm, w_edge_hbm, w_msg_hbm, w_out_hbm,
    pick, pick_t, act, a_node, recv_term, w_recv, w_self, w_edge, w_msg, w_out, sems,
):
    pairs = (
        (w_recv_hbm, w_recv), (w_self_hbm, w_self), (w_out_hbm, w_out), (w_edge_hbm, w_edge),
        (w_msg_hbm, w_msg), (a_node_hbm, a_node), (act_hbm, act),
    )
    copies = start_all(pairs, sems)
    edges = act.shape[0]
    nodes = 128
    rows = lax.broadcasted_iota(jnp.int32, (nodes, edges), 0)
    lanes = lax.broadcasted_iota(jnp.int32, (edges, nodes), 1)
    sends = jnp.broadcast_to(send_row[...], (nodes, edges))
    recvs = jnp.broadcast_to(recv_row[...], (nodes, edges))
    s_row = sends - rows
    s_col = jnp.transpose(sends) - lanes
    r_col = jnp.transpose(recvs)
    blocks = slot_blocks()
    for k, b in enumerate(blocks):
        pick[:, k * nodes : (k + 1) * nodes] = jnp.where(s_col == b * nodes, 1.0, 0.0).astype(BF)
        pick_t[k * nodes : (k + 1) * nodes, :] = jnp.where(s_row == b * nodes, 1.0, 0.0).astype(BF)
    k = len(blocks)
    pick[:, k * nodes :] = jnp.where(r_col == lanes, 1.0, 0.0).astype(BF)
    pick_t[k * nodes :, :] = jnp.where(recvs == rows, 1.0, 0.0).astype(BF)
    for copy in copies:
        copy.wait()
    d_bf = d[...].astype(BF)
    recv_term[...] = dot(d_bf, w_recv[...]).astype(BF)


def pass_kernel(block, after, out):
    out[...] = block[...]


def gathered(pick, first, parts, table):
    row = 0
    for part in parts:
        table[row : row + part.shape[0], :] = part[...]
        row += part.shape[0]
    return dot(pick[:, first : first + row], table[...])


def base_kernel(
    far, near, outer, inner, own, recv_term, pick, act, a_node, d, w_self, w_edge, w_msg, w_out,
    base, slope, node_slope, self_pre, d_back, fold, gram, table,
):
    d_bf = d[...].astype(BF)
    self_pre[...] = dot(d_bf, w_self[...])
    d_back[...] = dot_back(d_bf, w_out[...])
    fold[...] = dot(w_edge[...], w_msg[...]).astype(BF)
    gram[...] = dot_back(w_out[...], w_out[...]).astype(BF)
    slope[...] = silu_slope(act[...].astype(F32))
    node_slope[...] = silu_slope(a_node[...].astype(F32))
    base[...] = gathered(pick, 512, (near, far, outer, inner, own, recv_term), table)


def inner_kernel(far_inner, near_inner, base, pick, more, table):
    more[...] = base[...] + gathered(pick, 256, (far_inner, near_inner), table)


def lanes_of(row, width):
    nodes = row.shape[1]
    column = jnp.transpose(jnp.broadcast_to(row, (nodes, nodes)))
    return jnp.concatenate([column] * (width // nodes), axis=1)


def main_kernel(
    far_outer, near_outer, base, slope, pick, pick_t, node_slope, self_pre, fold, gram, d_back, obs,
    corner_outer, edge_grad, node_grad, node_hidden, table,
):
    edge_input = base[...] + gathered(pick, 0, (far_outer, near_outer), table)
    hidden = (slope[...] * edge_input).astype(BF)
    hidden_sum = dot(pick_t[1152:, :], hidden).astype(BF)
    pre_node = self_pre[...] + dot(hidden_sum, fold[...])
    inner = (node_slope[...] * pre_node).astype(BF)
    node_hidden[...] = inner
    back = lanes_of(obs[...], inner.shape[1]) * (d_back[...] + dot(inner, gram[...]))
    grad = (back * node_slope[...]).astype(BF)
    node_grad[...] = grad
    edge_back = dot_back(grad, fold[...]).astype(BF)
    e_grad = (dot(pick[:, 1152:], edge_back) * slope[...]).astype(BF)
    edge_grad[...] = e_grad
    corner_outer[...] = dot(pick_t[0:128, :], e_grad).astype(BF)


def corner_kernel(edge_grad, pick_t, corner_inner, all_near):
    sums = dot(pick_t[128:640, :], edge_grad[...]).astype(BF)
    corner_inner[...] = sums[128:256, :]
    all_near[0:128, :] = sums[0:128, :]
    all_near[128:384, :] = sums[256:512, :]


def rest_kernel(
    edge_grad, pick_t, node_grad, node_hidden, obs, d, w_recv, w_self, w_out,
    middle_far, mid, partial,
):
    sums = dot(pick_t[640:, :], edge_grad[...])
    middle_far[...] = sums[:128, :].astype(BF)
    mid[...] = sums[128:512, :]
    search = d[...]
    changed = search + dot(node_hidden[...], w_out[...])
    observed = lanes_of(obs[...], search.shape[1]) * changed
    back = dot_back(node_grad[...], w_self[...]) + dot_back(sums[512:, :].astype(BF), w_recv[...])
    partial[...] = search + observed + back


def merge_kernel(first, mid, from_far, from_near, *refs):
    rows = slice(first, first + 128)
    total = mid[rows, :] + from_far[...].astype(F32) + from_near[rows, :].astype(F32)
    refs[-1][...] = total.astype(BF)


def center_kernel(mid, from_outer, center):
    center[...] = mid[256:384, :] + from_outer[...].astype(F32)


def product_kernel(
    center, from_near, from_inner, from_far, partial, w_send, d, r, product, sums
):
    total = center[...] + from_near[256:384, :].astype(F32)
    for part in (from_far, from_inner):
        total = total + part[...].astype(F32)
    prod = partial[...] + dot_back(total.astype(BF), w_send[...])
    product[...] = prod
    res = r[...]
    lane = lax.broadcasted_iota(jnp.int32, sums.shape, 1)
    out = jnp.zeros(sums.shape, F32)
    for k, value in enumerate((res * res, d[...] * prod, res * prod, prod * prod)):
        out = jnp.where(lane == k, jnp.sum(value), out)
    sums[...] = out


def final_kernel(sums, x, r, d, product, new_x, new_r, new_d):
    total = jnp.sum(sums[...], axis=0, keepdims=True)
    norm_now, curvature = total[:, 0:1], total[:, 1:2]
    cross, square = total[:, 2:3], total[:, 3:4]
    alpha = norm_now / curvature
    norm_next = jnp.maximum(norm_now + alpha * (alpha * square - 2.0 * cross), 0.0)
    beta = norm_next / norm_now
    search = d[...]
    new_x[...] = x[...] + alpha * search
    left = r[...] - alpha * product[...]
    new_r[...] = left
    new_d[...] = left + beta * search


def swapped(value, axis, across):
    n_lat, n_lon = lax.axis_size("lat"), lax.axis_size("lon")

    def partner(i, j):
        if axis == "lon":
            return i, (j - 1 if j % 2 == 0 else j + 1) % n_lon if across else j ^ 1
        if not across:
            return i ^ 1, j
        return (i, j ^ 1) if i in (0, n_lat - 1) else (i - 1 if i % 2 == 0 else i + 1, j)

    pairs = []
    for i in range(n_lat):
        for j in range(n_lon):
            to_lat, to_lon = partner(i, j)
            pairs.append((i * n_lon + j, to_lat * n_lon + to_lon))
    return lax.ppermute(value, ("lat", "lon"), pairs)


def sums_everywhere(value):
    n_lat, n_lon = lax.axis_size("lat"), lax.axis_size("lon")
    near = n_lon // 4
    first = [
        [(2 * y + c) * n_lon + x * near + z for c in range(2) for z in range(near)]
        for y in range(n_lat // 2)
        for x in range(4)
    ]
    second = [
        [(2 * y + c) * n_lon + x * near + z for x in range(4) for y in range(n_lat // 2)]
        for c in range(2)
        for z in range(near)
    ]
    value = lax.all_to_all(value, ("lat", "lon"), 0, 0, tiled=True, axis_index_groups=first)
    value = jnp.sum(value, axis=0, keepdims=True)
    value = jnp.broadcast_to(value, (len(second[0]), value.shape[1]))
    return lax.all_to_all(value, ("lat", "lon"), 0, 0, tiled=True, axis_index_groups=second)


def body(
    x_field, residual, direction, a_node, a_edge, senders, receivers, obs_weight,
    w_send, w_recv, w_edge_out, w_node_self, w_node_msg, w_node_out,
):
    nodes, width = x_field.shape[2:]
    edges = a_edge.shape[2]
    x = x_field.reshape(nodes, width)
    r = residual.reshape(nodes, width)
    d_hbm = direction.reshape(nodes, width)
    field = shape(nodes, width, F32)
    block = shape(nodes, width, BF)
    weight = shape(width, width, BF)
    own, send_row, recv_row, obs, d = call(
        send_kernel,
        "send_term",
        (
            block,
            shape(1, edges, jnp.int32),
            shape(1, edges, jnp.int32),
            shape(1, nodes, F32),
            field,
        ),
        (senders.reshape(1, edges), receivers.reshape(1, edges), obs_weight.reshape(1, nodes), d_hbm, w_send),
        hbm=0,
        scratch=(pltpu.VMEM((width, width), BF), pltpu.SemaphoreType.DMA((5,))),
    )
    outer = swapped(own, "lon", True)
    inner = swapped(own, "lon", False)
    far = swapped(own, "lat", True)
    near = swapped(own, "lat", False)
    pick, pick_t, act, node_act, recv_term, w_recv, w_self, w_edge, w_msg, w_out = call(
        prepare_kernel,
        "prepare",
        (
            shape(edges, 10 * nodes, BF),
            shape(10 * nodes, edges, BF),
            shape(edges, width, BF),
            block,
            block,
        )
        + (weight,) * 5,
        (
            send_row, recv_row, d, a_edge.reshape(edges, width), a_node.reshape(nodes, width),
            w_recv, w_node_self, w_edge_out, w_node_msg, w_node_out,
        ),
        hbm=3,
        scratch=(
            pltpu.SemaphoreType.DMA((7,)),
        ),
    )
    pair = shape(2 * nodes, width, BF)
    inner = call(pass_kernel, "pass_inner", block, (inner, recv_term))
    far_inner = swapped(inner, "lat", True)
    near_inner = swapped(inner, "lat", False)
    outer = call(pass_kernel, "pass_outer", block, (outer, inner))
    far_outer = swapped(outer, "lat", True)
    near_outer = swapped(outer, "lat", False)
    base, slope, node_slope, self_pre, d_back, fold, gram = call(
        base_kernel,
        "base",
        (shape(edges, width, F32),) * 2 + (field, field, field, weight, weight),
        (far, near, outer, inner, own, recv_term, pick, act, node_act, d, w_self, w_edge, w_msg, w_out),
        scratch=(pltpu.VMEM((6 * nodes, width), BF),),
        cost=cost(LIGHT),
    )
    base = call(
        inner_kernel,
        "inner",
        shape(edges, width, F32),
        (far_inner, near_inner, base, pick),
        scratch=(pltpu.VMEM((2 * nodes, width), BF),),
        cost=cost(HEAVY),
    )
    far_outer = call(pass_kernel, "gate", block, (far_outer, base), cost=cost(HEAVY))
    corner_outer, edge_grad, node_grad, node_hidden = call(
        main_kernel,
        "main",
        (block, shape(edges, width, BF), block, block),
        (
            far_outer, near_outer, base, slope, pick, pick_t, node_slope, self_pre, fold, gram, d_back, obs,
        ),
        scratch=(pltpu.VMEM((2 * nodes, width), BF),),
    )
    far_outer = swapped(corner_outer, "lat", True)
    corner_inner, all_near = call(
        corner_kernel, "corner", (block, shape(3 * nodes, width, BF)), (edge_grad, pick_t)
    )
    far_inner = swapped(corner_inner, "lat", True)
    from_near = swapped(all_near, "lat", False)
    middle_far, mid, partial = call(
        rest_kernel,
        "rest",
        (block, shape(3 * nodes, width, F32), field),
        (edge_grad, pick_t, node_grad, node_hidden, obs, d, w_recv, w_self, w_out),
        cost=cost(LIGHT // 100),
    )
    far_outer = call(pass_kernel, "gate", block, (far_outer, obs), cost=cost(HEAVY))
    to_outer = call(
        functools.partial(merge_kernel, 0), "merge_outer", block, (mid, far_outer, from_near)
    )
    to_inner = call(
        functools.partial(merge_kernel, 128), "merge_inner", block, (mid, far_inner, from_near, to_outer)
    )
    from_outer = swapped(to_outer, "lon", True)
    from_inner = swapped(to_inner, "lon", False)
    from_far = swapped(middle_far, "lat", True)
    center = call(
        center_kernel,
        "center",
        field,
        (mid, from_outer),
        cost=cost(HEAVY),
    )
    product, sums = call(
        product_kernel,
        "product",
        (field, shape(16, 128, F32)),
        (center, from_near, from_inner, from_far, partial, w_send, d, r),
    )
    sums = sums_everywhere(sums)
    outs = call(final_kernel, "final", (field,) * 3, (sums, x, r, d, product))
    return tuple(out.reshape(x_field.shape) for out in outs)


def solution(mesh):
    field = P("lat", "lon", None, None)
    flat = P("lat", "lon", None)
    return jax.shard_map(
        body,
        mesh=mesh,
        in_specs=(field,) * 5 + (flat,) * 3 + (P(),) * 6,
        out_specs=(field,) * 3,
        check_vma=False,
    )
```

```python
import functools

import jax
import jax.numpy as jnp
from jax import lax
from jax.experimental import pallas as pl
from jax.experimental.pallas import tpu as pltpu
from jax.sharding import PartitionSpec as P

BF = jnp.bfloat16
F32 = jnp.float32
LIGHT = 10**9
HEAVY = 5 * 10**9
VMEM_LIMIT = 12 * 1024 * 1024


def dot(left, right):
    return jnp.dot(left, right, preferred_element_type=F32)


def dot_back(left, weight):
    return lax.dot_general(left, weight, (((1,), (1,)), ((), ())), preferred_element_type=F32)


def silu_slope(value):
    sig = 0.5 * jnp.tanh(0.5 * value) + 0.5
    return sig * (1.0 + value * (1.0 - sig))


def call(kernel, name, out_shape, args, scratch=(), hbm=None, cost=None):
    here = pl.BlockSpec(memory_space=pltpu.VMEM)
    there = pl.BlockSpec(memory_space=pltpu.HBM)
    first = len(args) if hbm is None else hbm
    away = [pltpu.with_memory_space_constraint(arg, pltpu.HBM) for arg in args[first:]]
    return pl.pallas_call(
        kernel,
        out_shape=out_shape,
        in_specs=[here] * first + [there] * len(away),
        out_specs=jax.tree.map(lambda _: here, out_shape),
        scratch_shapes=scratch,
        compiler_params=pltpu.CompilerParams(vmem_limit_bytes=VMEM_LIMIT),
        cost_estimate=cost,
        name=name,
    )(*args[:first], *away)


def cost(flops):
    return pl.CostEstimate(flops=flops, bytes_accessed=flops // 100, transcendentals=0)


def shape(rows, cols, kind):
    return jax.ShapeDtypeStruct((rows, cols), kind)


def start_all(pairs, sems):
    copies = [pltpu.make_async_copy(a, b, sems.at[k]) for k, (a, b) in enumerate(pairs)]
    for copy in copies:
        copy.start()
    return copies


def slot_blocks():
    near = 1 - 2 * lax.rem(lax.axis_index("lat"), 2)
    inner = 1 - 2 * lax.rem(lax.axis_index("lon"), 2)
    places = (
        (-near, -inner), (near, -inner), (-near, inner), (near, inner), (near, 0), (-near, 0),
        (0, -inner), (0, inner), (0, 0),
    )
    return [(lat + 1) * 3 + lon + 1 for lat, lon in places]


def send_kernel(senders, receivers, obs_hbm, d_hbm, w_hbm, own, send_row, recv_row, obs, d, w, sems):
    pairs = ((d_hbm, d), (w_hbm, w), (senders, send_row), (receivers, recv_row), (obs_hbm, obs))
    for copy in start_all(pairs, sems):
        copy.wait()
    own[...] = dot(d[...].astype(BF), w[...]).astype(BF)


def prepare_kernel(
    send_row, recv_row, d, act_hbm, a_node_hbm, w_recv_hbm, w_self_hbm, w_edge_hbm, w_msg_hbm, w_out_hbm,
    pick, pick_t, act, a_node, recv_term, w_recv, w_self, w_edge, w_msg, w_out, sems,
):
    pairs = (
        (w_recv_hbm, w_recv), (w_self_hbm, w_self), (w_out_hbm, w_out), (w_edge_hbm, w_edge),
        (w_msg_hbm, w_msg), (a_node_hbm, a_node), (act_hbm, act),
    )
    copies = start_all(pairs, sems)
    edges = act.shape[0]
    nodes = 128
    rows = lax.broadcasted_iota(jnp.int32, (nodes, edges), 0)
    lanes = lax.broadcasted_iota(jnp.int32, (edges, nodes), 1)
    sends = jnp.broadcast_to(send_row[...], (nodes, edges))
    recvs = jnp.broadcast_to(recv_row[...], (nodes, edges))
    s_row = sends - rows
    s_col = jnp.transpose(sends) - lanes
    r_col = jnp.transpose(recvs)
    blocks = slot_blocks()
    for k, b in enumerate(blocks):
        pick[:, k * nodes : (k + 1) * nodes] = jnp.where(s_col == b * nodes, 1.0, 0.0).astype(BF)
        pick_t[k * nodes : (k + 1) * nodes, :] = jnp.where(s_row == b * nodes, 1.0, 0.0).astype(BF)
    k = len(blocks)
    pick[:, k * nodes :] = jnp.where(r_col == lanes, 1.0, 0.0).astype(BF)
    pick_t[k * nodes :, :] = jnp.where(recvs == rows, 1.0, 0.0).astype(BF)
    for copy in copies:
        copy.wait()
    d_bf = d[...].astype(BF)
    recv_term[...] = dot(d_bf, w_recv[...]).astype(BF)


def pass_kernel(block, after, out):
    out[...] = block[...]


def gathered(pick, first, parts, table):
    row = 0
    for part in parts:
        table[row : row + part.shape[0], :] = part[...]
        row += part.shape[0]
    return dot(pick[:, first : first + row], table[...])


def base_kernel(
    far, near, outer, inner, own, recv_term, pick, act, a_node, d, w_self, w_edge, w_msg, w_out,
    base, slope, node_slope, self_pre, d_back, fold, gram, table,
):
    d_bf = d[...].astype(BF)
    self_pre[...] = dot(d_bf, w_self[...])
    d_back[...] = dot_back(d_bf, w_out[...])
    fold[...] = dot(w_edge[...], w_msg[...]).astype(BF)
    gram[...] = dot_back(w_out[...], w_out[...]).astype(BF)
    slope[...] = silu_slope(act[...].astype(F32))
    node_slope[...] = silu_slope(a_node[...].astype(F32))
    base[...] = gathered(pick, 512, (near, far, outer, inner, own, recv_term), table)


def inner_kernel(far_inner, near_inner, base, pick, more, table):
    more[...] = base[...] + gathered(pick, 256, (far_inner, near_inner), table)


def lanes_of(row, width):
    nodes = row.shape[1]
    column = jnp.transpose(jnp.broadcast_to(row, (nodes, nodes)))
    return jnp.concatenate([column] * (width // nodes), axis=1)


def main_kernel(
    far_outer, near_outer, base, slope, pick, pick_t, node_slope, self_pre, fold, gram, d_back, obs,
    corner_outer, edge_grad, node_grad, node_hidden, table,
):
    edge_input = base[...] + gathered(pick, 0, (far_outer, near_outer), table)
    hidden = (slope[...] * edge_input).astype(BF)
    hidden_sum = dot(pick_t[1152:, :], hidden).astype(BF)
    pre_node = self_pre[...] + dot(hidden_sum, fold[...])
    inner = (node_slope[...] * pre_node).astype(BF)
    node_hidden[...] = inner
    back = lanes_of(obs[...], inner.shape[1]) * (d_back[...] + dot(inner, gram[...]))
    grad = (back * node_slope[...]).astype(BF)
    node_grad[...] = grad
    edge_back = dot_back(grad, fold[...]).astype(BF)
    e_grad = (dot(pick[:, 1152:], edge_back) * slope[...]).astype(BF)
    edge_grad[...] = e_grad
    corner_outer[...] = dot(pick_t[0:128, :], e_grad).astype(BF)


def corner_kernel(edge_grad, pick_t, corner_inner, all_near):
    sums = dot(pick_t[128:640, :], edge_grad[...]).astype(BF)
    corner_inner[...] = sums[128:256, :]
    all_near[0:128, :] = sums[0:128, :]
    all_near[128:384, :] = sums[256:512, :]


def rest_kernel(
    edge_grad, pick_t, node_grad, node_hidden, obs, d, w_recv, w_self, w_out,
    middle_far, mid, partial,
):
    sums = dot(pick_t[640:, :], edge_grad[...])
    middle_far[...] = sums[:128, :].astype(BF)
    mid[...] = sums[128:512, :]
    search = d[...]
    changed = search + dot(node_hidden[...], w_out[...])
    observed = lanes_of(obs[...], search.shape[1]) * changed
    back = dot_back(node_grad[...], w_self[...]) + dot_back(sums[512:, :].astype(BF), w_recv[...])
    partial[...] = search + observed + back


def merge_kernel(first, mid, from_far, from_near, *refs):
    rows = slice(first, first + 128)
    total = mid[rows, :] + from_far[...].astype(F32) + from_near[rows, :].astype(F32)
    refs[-1][...] = total.astype(BF)


def center_kernel(mid, from_outer, center):
    center[...] = mid[256:384, :] + from_outer[...].astype(F32)


def product_kernel(
    center, from_near, from_inner, from_far, partial, w_send, d, r, product, sums
):
    total = center[...] + from_near[256:384, :].astype(F32)
    for part in (from_far, from_inner):
        total = total + part[...].astype(F32)
    prod = partial[...] + dot_back(total.astype(BF), w_send[...])
    product[...] = prod
    res = r[...]
    row = lax.broadcasted_iota(jnp.int32, (8, 128), 0)
    lane = lax.broadcasted_iota(jnp.int32, (8, 128), 1)
    folds = jnp.zeros((8, 128), F32)
    for k, value in enumerate((res * res, d[...] * prod, res * prod, prod * prod)):
        fold = jnp.sum(value, axis=0, keepdims=True)
        fold = fold[:, 0:128] + fold[:, 128:256] + fold[:, 256:384] + fold[:, 384:512]
        folds = jnp.where(row == k, fold, folds)
    spread = jnp.where(row == lane, jnp.sum(folds, axis=1, keepdims=True), 0.0)
    sums[...] = jnp.broadcast_to(jnp.sum(spread, axis=0, keepdims=True), sums.shape)


def final_kernel(sums, x, r, d, product, new_x, new_r, new_d):
    total = jnp.sum(sums[...], axis=0, keepdims=True)
    norm_now, curvature = total[:, 0:1], total[:, 1:2]
    cross, square = total[:, 2:3], total[:, 3:4]
    alpha = norm_now / curvature
    norm_next = jnp.maximum(norm_now + alpha * (alpha * square - 2.0 * cross), 0.0)
    beta = norm_next / norm_now
    search = d[...]
    new_x[...] = x[...] + alpha * search
    left = r[...] - alpha * product[...]
    new_r[...] = left
    new_d[...] = left + beta * search


def swapped(value, axis, across):
    n_lat, n_lon = lax.axis_size("lat"), lax.axis_size("lon")

    def partner(i, j):
        if axis == "lon":
            return i, (j - 1 if j % 2 == 0 else j + 1) % n_lon if across else j ^ 1
        if not across:
            return i ^ 1, j
        return (i, j ^ 1) if i in (0, n_lat - 1) else (i - 1 if i % 2 == 0 else i + 1, j)

    pairs = []
    for i in range(n_lat):
        for j in range(n_lon):
            to_lat, to_lon = partner(i, j)
            pairs.append((i * n_lon + j, to_lat * n_lon + to_lon))
    return lax.ppermute(value, ("lat", "lon"), pairs)


def sums_everywhere(value):
    n_lat, n_lon = lax.axis_size("lat"), lax.axis_size("lon")
    near = n_lon // 4
    first = [
        [(2 * y + c) * n_lon + x * near + z for c in range(2) for z in range(near)]
        for y in range(n_lat // 2)
        for x in range(4)
    ]
    second = [
        [(2 * y + c) * n_lon + x * near + z for y in range(n_lat // 2) for x in range(4)]
        for c in range(2)
        for z in range(near)
    ]
    value = lax.all_to_all(value, ("lat", "lon"), 0, 0, tiled=True, axis_index_groups=first)
    value = jnp.sum(value, axis=0, keepdims=True)
    value = jnp.broadcast_to(value, (len(second[0]), value.shape[1]))
    return lax.all_to_all(value, ("lat", "lon"), 0, 0, tiled=True, axis_index_groups=second)


def body(
    x_field, residual, direction, a_node, a_edge, senders, receivers, obs_weight,
    w_send, w_recv, w_edge_out, w_node_self, w_node_msg, w_node_out,
):
    nodes, width = x_field.shape[2:]
    edges = a_edge.shape[2]
    x = x_field.reshape(nodes, width)
    r = residual.reshape(nodes, width)
    d_hbm = direction.reshape(nodes, width)
    field = shape(nodes, width, F32)
    block = shape(nodes, width, BF)
    weight = shape(width, width, BF)
    own, send_row, recv_row, obs, d = call(
        send_kernel,
        "send_term",
        (
            block,
            shape(1, edges, jnp.int32),
            shape(1, edges, jnp.int32),
            shape(1, nodes, F32),
            field,
        ),
        (senders.reshape(1, edges), receivers.reshape(1, edges), obs_weight.reshape(1, nodes), d_hbm, w_send),
        hbm=0,
        scratch=(pltpu.VMEM((width, width), BF), pltpu.SemaphoreType.DMA((5,))),
    )
    outer = swapped(own, "lon", True)
    inner = swapped(own, "lon", False)
    far = swapped(own, "lat", True)
    near = swapped(own, "lat", False)
    pick, pick_t, act, node_act, recv_term, w_recv, w_self, w_edge, w_msg, w_out = call(
        prepare_kernel,
        "prepare",
        (
            shape(edges, 10 * nodes, BF),
            shape(10 * nodes, edges, BF),
            shape(edges, width, BF),
            block,
            block,
        )
        + (weight,) * 5,
        (
            send_row, recv_row, d, a_edge.reshape(edges, width), a_node.reshape(nodes, width),
            w_recv, w_node_self, w_edge_out, w_node_msg, w_node_out,
        ),
        hbm=3,
        scratch=(
            pltpu.SemaphoreType.DMA((7,)),
        ),
    )
    pair = shape(2 * nodes, width, BF)
    inner = call(pass_kernel, "pass_inner", block, (inner, recv_term))
    far_inner = swapped(inner, "lat", True)
    near_inner = swapped(inner, "lat", False)
    outer = call(pass_kernel, "pass_outer", block, (outer, inner))
    far_outer = swapped(outer, "lat", True)
    near_outer = swapped(outer, "lat", False)
    base, slope, node_slope, self_pre, d_back, fold, gram = call(
        base_kernel,
        "base",
        (shape(edges, width, F32),) * 2 + (field, field, field, weight, weight),
        (far, near, outer, inner, own, recv_term, pick, act, node_act, d, w_self, w_edge, w_msg, w_out),
        scratch=(pltpu.VMEM((6 * nodes, width), BF),),
        cost=cost(LIGHT),
    )
    base = call(
        inner_kernel,
        "inner",
        shape(edges, width, F32),
        (far_inner, near_inner, base, pick),
        scratch=(pltpu.VMEM((2 * nodes, width), BF),),
        cost=cost(HEAVY),
    )
    far_outer = call(pass_kernel, "gate", block, (far_outer, base), cost=cost(HEAVY))
    corner_outer, edge_grad, node_grad, node_hidden = call(
        main_kernel,
        "main",
        (block, shape(edges, width, BF), block, block),
        (
            far_outer, near_outer, base, slope, pick, pick_t, node_slope, self_pre, fold, gram, d_back, obs,
        ),
        scratch=(pltpu.VMEM((2 * nodes, width), BF),),
    )
    far_outer = swapped(corner_outer, "lat", True)
    corner_inner, all_near = call(
        corner_kernel, "corner", (block, shape(3 * nodes, width, BF)), (edge_grad, pick_t)
    )
    far_inner = swapped(corner_inner, "lat", True)
    from_near = swapped(all_near, "lat", False)
    middle_far, mid, partial = call(
        rest_kernel,
        "rest",
        (block, shape(3 * nodes, width, F32), field),
        (edge_grad, pick_t, node_grad, node_hidden, obs, d, w_recv, w_self, w_out),
        cost=cost(LIGHT // 100),
    )
    far_outer = call(pass_kernel, "gate", block, (far_outer, obs), cost=cost(HEAVY))
    to_outer = call(
        functools.partial(merge_kernel, 0), "merge_outer", block, (mid, far_outer, from_near)
    )
    to_inner = call(
        functools.partial(merge_kernel, 128), "merge_inner", block, (mid, far_inner, from_near, to_outer)
    )
    from_outer = swapped(to_outer, "lon", True)
    from_inner = swapped(to_inner, "lon", False)
    from_far = swapped(middle_far, "lat", True)
    center = call(
        center_kernel,
        "center",
        field,
        (mid, from_outer),
        cost=cost(HEAVY),
    )
    product, sums = call(
        product_kernel,
        "product",
        (field, shape(16, 128, F32)),
        (center, from_near, from_inner, from_far, partial, w_send, d, r),
    )
    sums = sums_everywhere(sums)
    outs = call(final_kernel, "final", (field,) * 3, (sums, x, r, d, product))
    return tuple(out.reshape(x_field.shape) for out in outs)


def solution(mesh):
    field = P("lat", "lon", None, None)
    flat = P("lat", "lon", None)
    return jax.shard_map(
        body,
        mesh=mesh,
        in_specs=(field,) * 5 + (flat,) * 3 + (P(),) * 6,
        out_specs=(field,) * 3,
        check_vma=False,
    )
```
